256 devices in a mesh: grp: 4 (over y), blk: 64 (over z, x, core).
Axes of the slice: x: 4, y: 4, z: 8, core: 2. Of those that a mesh axis runs over, the one named last changes fastest.
Arguments:
- coeffs: bfloat16 [2, 2048, 1024], P(None, ('grp', 'blk')), may hold values from -6 to 6
- coupling: int32 [4, 4], replicated, may hold values from -1 to 1, as said below
- one_body: float32 [4, 4, 2, 64, 64], P('grp', None, None, 'blk'), may hold values from -0.125 to 0.125
- target_orb: int32 [131072], P(('grp', 'blk')), may hold values from 0 to 63
- source_orb: int32 [2048], replicated, may hold values from 0 to 63
- excite: int32 [131072, 2048], P(('grp', 'blk')), may hold values from -1 to 1
- live_rows: int32 [256], P(('grp', 'blk')), may hold values from 1 to 512, 98304 in all
Outputs:
- sigma: float32 [2, 131072, 1024], P(None, ('grp', 'blk'))
The draws below stay inside these ranges and needn't reach their ends.
Inputs may be any that keep to these rules, and one draw needn't show every extreme that they name: `coupling`: Symmetric, with ones on the diagonal and entries of 1 or -1 elsewhere. `live_rows`: some block has all 512 strings live.
All inputs are finite; a program needn't handle non-finite values.
Results may differ from the reference program's by a relative error of at most 0.0029.
Values may be sent and summed in bfloat16 or wider, within the bound.
No kernel may reach another device: no remote copies, remote signals or barrier semaphores. Data moves between devices by JAX's collectives and lax.ppermute only.
A program may use at most 128 MiB of HBM per device.

```python
import math
import jax
import jax.numpy as jnp
import numpy as np
from jax import lax

NORB = 64
RT = 512
RS = 8
B = 1024
GROUPS = 4
SIGMA_ROWS = 131072
SOURCE_ROWS = 2048
N_GRP = 4
N_BLK = 64


def draw_coupling(key, part):
    key = jax.random.fold_in(key, 11)
    upper = 2 * jax.random.randint(key, (N_GRP, N_GRP), 0, 2) - 1
    strict = jnp.triu(upper, 1)
    return (strict + strict.T + jnp.eye(N_GRP, dtype=jnp.int32)).astype(jnp.int32)


def plant(drawn, own_key, low, largest):
    spot = [jax.random.randint(jax.random.fold_in(own_key, axis), (), 0, length) for axis, length in enumerate(drawn.shape)]
    main_axis = drawn.shape.index(max(drawn.shape))
    neighbour = spot[:main_axis] + [(spot[main_axis] + 1) % drawn.shape[main_axis]] + spot[main_axis + 1:]
    return drawn.at[tuple(spot)].set(low).at[tuple(neighbour)].set(largest)


def shard_levels(stream_key, dims, shards, smallest, largest):
    loudness = 1.0
    for dim, blocks in shards:
        steps = jax.random.uniform(jax.random.fold_in(jax.random.fold_in(stream_key, 6), dim), (blocks,), jnp.float32, smallest / len(shards), largest / len(shards))
        loudness = loudness * jnp.repeat(jnp.exp(steps), dims[dim] // blocks).reshape((-1,) + (1,) * (len(dims) - 1 - dim))
    return loudness


def profile(number_of, total, most, skew):
    loads = [(1 << 20) // math.isqrt(standing ** skew) + 1 for standing in range(2, number_of + 1)]
    surplus, given = total - most - (number_of - 1), [1] * (number_of - 1)
    while surplus > 0:
        movable = [i for i in range(number_of - 1) if given[i] < most]
        mass, remaining = sum([loads[i] for i in movable]), surplus
        for i in movable:
            more = min(most - given[i], max(1, remaining * loads[i] // mass), surplus)
            given[i] = given[i] + more
            surplus = surplus - more
    return np.array([most] + given)


def uneven(rng, amount, total, reach, skew):
    if amount == 2:
        one = jax.random.randint(rng, (), max(1, total - reach), min(reach, total - 1) + 1)
        return jnp.stack([one, total - one])
    tallies = jnp.asarray(profile(amount, total, reach, skew), jnp.int32)
    twos = (amount - 1) // 2
    donor, sink = tallies[1:1 + 2 * twos:2], tallies[2:2 + 2 * twos:2]
    room = jnp.minimum(donor - 1, reach - sink)
    shifted = jax.random.randint(jax.random.fold_in(rng, 1), (twos,), 0, 1 << 20) % (room + 1)
    tallies = tallies.at[1:1 + 2 * twos:2].set(donor - shifted).at[2:2 + 2 * twos:2].set(sink + shifted)
    return tallies[jax.random.permutation(jax.random.fold_in(rng, 2), amount)]


def gaussian(key, dims, scale, most, cuts=(), kind=jnp.bfloat16):
    level = shard_levels(key, dims, cuts, -0.22, 0.18) if cuts else 1.0
    entries = jax.random.normal(key, dims, jnp.float32) * scale * level
    return jnp.minimum(jnp.maximum(entries, -most), most).astype(kind)


def setup_inputs(seed: int = 0) -> dict:
    keys = jax.random.split(jax.random.key(seed), 8)
    coeffs = gaussian(keys[0], (2, SOURCE_ROWS, B), 1.0, 6.0, ((1, 256),))
    coupling = draw_coupling(jax.random.fold_in(keys[7], 71), 0)
    one_body = gaussian(keys[2], (GROUPS, GROUPS, 2, NORB, NORB), SOURCE_ROWS ** -0.5, 0.125, ((0, 4), (3, 64)), jnp.float32)
    target_orb = plant(jax.random.randint(keys[3], (SIGMA_ROWS,), 0, NORB), jax.random.fold_in(keys[3], 1), 0, NORB - 1).astype(jnp.int32)
    source_orb = plant(jax.random.randint(keys[4], (SOURCE_ROWS,), 0, NORB), jax.random.fold_in(keys[4], 1), 0, NORB - 1).astype(jnp.int32)
    excite = plant(jax.random.randint(keys[5], (SIGMA_ROWS, SOURCE_ROWS), -1, 2), jax.random.fold_in(keys[5], 1), -1, 1).astype(jnp.int32)
    live_rows = uneven(keys[6], N_GRP * N_BLK, N_GRP * N_BLK * RT * 3 // 4, RT, 2).astype(jnp.int32)
    return dict(coeffs=coeffs, coupling=coupling, one_body=one_body, target_orb=target_orb, source_orb=source_orb, excite=excite, live_rows=live_rows)


highest = lax.Precision.HIGHEST


def reference(coeffs, coupling, one_body, target_orb, source_orb, excite, live_rows):
    per_group = N_BLK * RS
    labels = jnp.arange(NORB, dtype=jnp.int32)
    source_hot = (source_orb.reshape(N_GRP, per_group)[:, :, None] == labels[None, None, :]).astype(jnp.float32)
    columns = coeffs.astype(jnp.float32).reshape(2, N_GRP, per_group, B)

    def one_block(block):
        group = block // N_BLK
        rows = lax.dynamic_slice_in_dim(target_orb, block * RT, RT)
        target_hot = (rows[:, None] == labels[None, :]).astype(jnp.float32)
        tables = lax.dynamic_index_in_dim(one_body, group, 0, keepdims=False)
        rowwise = jnp.einsum("im,gcmn->cgin", target_hot, tables, precision=highest)
        lookup = jnp.einsum("cgin,gjn->cigj", rowwise, source_hot, precision=highest)
        signs = lax.dynamic_slice_in_dim(excite, block * RT, RT, 0).reshape(RT, N_GRP, per_group).astype(jnp.float32)
        couple_row = lax.dynamic_index_in_dim(coupling, group, 0, keepdims=False).astype(jnp.float32)
        operator = (lookup * signs[None] * couple_row[None, None, :, None]).astype(jnp.bfloat16).astype(jnp.float32)
        real_sum = jnp.einsum("igj,gjb->ib", operator[0], columns[0]) - jnp.einsum("igj,gjb->ib", operator[1], columns[1])
        imag_sum = jnp.einsum("igj,gjb->ib", operator[0], columns[1]) + jnp.einsum("igj,gjb->ib", operator[1], columns[0])
        live = jnp.arange(RT, dtype=jnp.int32) < live_rows[block]
        result = jnp.stack([real_sum, imag_sum])
        return jnp.where(live[None, :, None], result, jnp.zeros_like(result))

    blocks = lax.map(one_block, jnp.arange(N_GRP * N_BLK, dtype=jnp.int32))
    return jnp.transpose(blocks, (1, 0, 2, 3)).reshape(2, N_GRP * N_BLK * RT, B)
```

```python
import functools

import jax
import jax.numpy as jnp
import numpy as np
from jax import lax
from jax.experimental import pallas as pl
from jax.experimental.pallas import tpu as pltpu

NY, NZ, NX = 4, 8, 4
AXES = ("grp", "blk")
STAGES = (
    ((0, 0, 4),),
    ((2, 0, 1), (0, 0, 2), (2, 0, -1)),
    ((0, 1, 1), (0, 2, 0), (0, -1, 1)),
    ((1, 0, 0), (-1, 0, 0), (0, 0, 1)),
)
HERE = ((0, 0, 0),)
SWAP = [(i, i ^ 1) for i in range(NY * NZ * NX * 2)]
MIB = 1 << 20


def mirrored(o):
    return (o[1], o[0], -o[2])


def index(x, y, z, c):
    return ((y % NY * NZ + z % NZ) * NX + x % NX) * 2 + c


def route(offset):
    pairs = []
    for y in range(NY):
        for z in range(NZ):
            for x in range(NX):
                for c in range(2):
                    dx, dy, dz = mirrored(offset) if c else offset
                    pairs.append((index(x + dx, y + dy, z + dz, c), index(x, y, z, c)))
    return pairs


def fetch(block, stage):
    return [lax.ppermute(block, AXES, route(o)) for o in STAGES[stage]]


def swap(block):
    return lax.ppermute(block, AXES, SWAP)


def chunk_offsets(last, half):
    second = HERE + STAGES[2]
    out = []
    for o2 in second[2 * half : 2 * half + 2]:
        for o1 in HERE + STAGES[1]:
            for o0 in HERE + STAGES[0]:
                out.append([sum(t) for t in zip(last, o2, o1, o0)])
    return out


def order_constants():
    lasts = HERE + STAGES[3]
    chunks = [(lasts[0], h, s) for s in (0, 1) for h in (0, 1)]
    for h in (0, 1):
        chunks += [(o, h, s) for s in (0, 1) for o in lasts[1:]]
    table = np.zeros((2, 5, len(chunks) * 128), np.int32)
    for core in (0, 1):
        at = 0
        for last, half, sibling in chunks:
            owner = core ^ sibling
            for o in chunk_offsets(last, half):
                dx, dy, dz = mirrored(o) if owner else o
                table[core, :, at : at + 8] = np.array([[dx], [dy], [dz], [owner], [0]])
                table[core, 4, at : at + 8] = np.arange(8)
                at += 8
    return table


ORDER = order_constants()


def operator_kernel(order_ref, aux_ref, target_ref, table_ref, excite_ref, out_ref, signs, rows):
    @pl.when(pl.program_id(0) == 0)
    def _():
        signs[:512, :] = excite_ref[...].astype(jnp.float32).astype(jnp.bfloat16)
        signs[512:, :] = aux_ref[...].astype(jnp.bfloat16)
        labels = lax.broadcasted_iota(jnp.int32, (64, 512), 0)
        hot = (labels == target_ref[...]).astype(jnp.float32).astype(jnp.bfloat16)
        rows[...] = lax.dot_general(
            hot, table_ref[...], (((0,), (0,)), ((), ())), preferred_element_type=jnp.float32
        ).astype(jnp.bfloat16)

    width = order_ref.shape[1]
    place = lax.broadcasted_iota(jnp.int32, (2048, width), 0)
    move = (place == order_ref[...]).astype(jnp.float32).astype(jnp.bfloat16)
    moved = jnp.dot(signs[...], move, preferred_element_type=jnp.float32)
    label = moved[512:513, :].astype(jnp.int32)
    couple = moved[513:514, :]
    lines = lax.broadcasted_iota(jnp.int32, (256, width), 0)
    hot = jnp.where(lines == label, couple, 0.0).astype(jnp.bfloat16)
    sign = moved[:512, :]
    for part in range(2):
        look = jnp.dot(rows[:, part * 256 : part * 256 + 256], hot, preferred_element_type=jnp.float32)
        value = (look * sign).astype(jnp.bfloat16)
        for piece in range(width // 128):
            at = piece * 256 + part * 128
            out_ref[:, at : at + 128] = value[:, piece * 128 : piece * 128 + 128]


def build_operator(order, aux, target, table, excite, width=256):
    columns = order.shape[1]
    return pl.pallas_call(
        operator_kernel,
        grid=(columns // width,),
        in_specs=[
            pl.BlockSpec((1, width), lambda i: (0, i)),
            pl.BlockSpec((16, 2048), lambda i: (0, 0)),
            pl.BlockSpec((1, 512), lambda i: (0, 0)),
            pl.BlockSpec((64, 512), lambda i: (0, 0)),
            pl.BlockSpec((512, 2048), lambda i: (0, 0)),
        ],
        out_specs=pl.BlockSpec((512, 2 * width), lambda i: (0, i)),
        out_shape=jax.ShapeDtypeStruct((512, 2 * columns), jnp.bfloat16),
        scratch_shapes=[pltpu.VMEM((528, 2048), jnp.bfloat16), pltpu.VMEM((512, 512), jnp.bfloat16)],
        compiler_params=pltpu.CompilerParams(vmem_limit_bytes=32 * MIB),
        cost_estimate=pl.CostEstimate(
            flops=2 * 512 * columns * 2560, bytes_accessed=4 * MIB + 2048 * columns, transcendentals=0
        ),
    )(order, aux, target, table, excite)


def product_kernel(first, last, count, *refs):
    live_ref, left_ref = refs[:2]
    chunks = refs[2 : 2 + count]
    total_ref = None if first else refs[2 + count]
    out_ref = refs[-1]

    def run(signs):
        acc = jnp.zeros((512, out_ref.shape[2]), jnp.float32) if first else total_ref[0]
        for k, chunk in enumerate(chunks):
            for half, (part, negative) in enumerate(signs):
                right = chunk[part]
                if negative:
                    right = -right
                at = k * 256 + half * 128
                acc = acc + jnp.dot(left_ref[:, at : at + 128], right, preferred_element_type=jnp.float32)
        if last:
            line = lax.broadcasted_iota(jnp.int32, acc.shape, 0)
            acc = jnp.where(line < live_ref[0], acc, 0.0)
        out_ref[0] = acc

    @pl.when(pl.program_id(0) == 0)
    def _():
        run(((0, False), (1, True)))

    @pl.when(pl.program_id(0) == 1)
    def _():
        run(((1, False), (0, False)))


def product(live, left, chunks, total, last, width=512):
    count = len(chunks)
    first = total is None
    block = pl.BlockSpec((1, 512, width), lambda p, n: (p, 0, n))
    return pl.pallas_call(
        functools.partial(product_kernel, first, last, count),
        grid=(2, 1024 // width),
        in_specs=[
            pl.BlockSpec(memory_space=pltpu.SMEM),
            pl.BlockSpec((512, 256 * count), lambda p, n: (0, 0)),
        ]
        + [pl.BlockSpec((2, 128, width), lambda p, n: (0, 0, n))] * count
        + ([] if first else [block]),
        out_specs=block,
        out_shape=jax.ShapeDtypeStruct((2, 512, 1024), jnp.float32),
        input_output_aliases={} if first else {2 + count: 0},
        compiler_params=pltpu.CompilerParams(vmem_limit_bytes=32 * MIB),
        cost_estimate=pl.CostEstimate(
            flops=2 * 512 * 1024 * 512 * count, bytes_accessed=(12 + count) * MIB, transcendentals=0
        ),
    )(live, left, *chunks, *([] if first else [total]))


def on_device(coeffs, coupling, one_body, target_orb, source_orb, excite, live_rows):
    grp, blk = lax.axis_index("grp"), lax.axis_index("blk")
    y, z, x, core = grp, blk // 8, blk // 2 % 4, blk % 2

    slab = jnp.concatenate([coeffs] + fetch(coeffs, 0), 1)

    row = one_body[0, :, :, 0, :].astype(jnp.bfloat16).transpose(1, 0, 2).reshape(1, 4, 128)
    table = lax.all_to_all(jnp.broadcast_to(row, (64, 4, 128)), "blk", 0, 0, tiled=True).reshape(64, 512)

    dx, dy, dz, owner, place = jnp.where(core == 0, ORDER[0], ORDER[1])
    order = ((((y + dy) % NY * NZ + (z + dz) % NZ) * NX + (x + dx) % NX) * 2 + owner) * 8 + place
    order = order[None, :]
    group = jnp.arange(2048, dtype=jnp.int32) // 512
    label = group * 64 + source_orb
    couple = jnp.repeat(lax.dynamic_index_in_dim(coupling, grp, 0, keepdims=False), 512)
    aux = jnp.concatenate([label[None], couple[None], jnp.zeros((14, 2048), jnp.int32)]).astype(jnp.float32)
    target = target_orb[None, :]
    build = functools.partial(build_operator, aux=aux, target=target, table=table, excite=excite)
    left0, left1, left2 = build(order[:, :512]), build(order[:, 512:1280]), build(order[:, 1280:])

    slab = jnp.concatenate([slab] + fetch(slab, 1), 1)
    near = fetch(slab, 2)
    halves = [jnp.concatenate([slab, near[0]], 1), jnp.concatenate(near[1:], 1)]
    total = product(live_rows, left0, halves + [swap(h) for h in halves], None, False)
    for half, left, last in ((halves[0], left1, False), (halves[1], left2, True)):
        got = fetch(half, 3)
        total = product(live_rows, left, got + [swap(g) for g in got], total, last)
    return total


def solution(mesh):
    from jax.sharding import PartitionSpec as P

    return jax.shard_map(
        on_device,
        mesh=mesh,
        in_specs=(
            P(None, ("grp", "blk"), None),
            P(),
            P("grp", None, None, "blk", None),
            P(("grp", "blk")),
            P(),
            P(("grp", "blk"), None),
            P(("grp", "blk")),
        ),
        out_specs=P(None, ("grp", "blk"), None),
        check_vma=False,
    )
```

```python
import functools

import jax
import jax.numpy as jnp
import numpy as np
from jax import lax
from jax.experimental import pallas as pl
from jax.experimental.pallas import tpu as pltpu

NY, NZ, NX = 4, 8, 4
AXES = ("grp", "blk")
STAGES = (
    ((0, 0, 4),),
    ((2, 0, 1), (0, 0, 2), (2, 0, -1)),
    ((0, 1, 1), (0, 2, 0), (0, -1, 1)),
    ((1, 0, 0), (-1, 0, 0), (0, 0, 1)),
)
HERE = ((0, 0, 0),)
SWAP = [(i, i ^ 1) for i in range(NY * NZ * NX * 2)]
MIB = 1 << 20


def mirrored(o):
    return (o[1], o[0], -o[2])


def index(x, y, z, c):
    return ((y % NY * NZ + z % NZ) * NX + x % NX) * 2 + c


def route(offset):
    pairs = []
    for y in range(NY):
        for z in range(NZ):
            for x in range(NX):
                for c in range(2):
                    dx, dy, dz = mirrored(offset) if c else offset
                    pairs.append((index(x + dx, y + dy, z + dz, c), index(x, y, z, c)))
    return pairs


def fetch(block, stage):
    return [lax.ppermute(block, AXES, route(o)) for o in STAGES[stage]]


def swap(block):
    return lax.ppermute(block, AXES, SWAP)


def half_offsets(last, half):
    second = HERE + STAGES[2]
    out = []
    for o2 in second[2 * half : 2 * half + 2]:
        for o1 in HERE + STAGES[1]:
            for o0 in HERE + STAGES[0]:
                out.append([sum(t) for t in zip(last, o2, o1, o0)])
    return out


def order_constants():
    lasts = HERE + STAGES[3]
    own = [(lasts[0], 0), (lasts[0], 1)] + [(o, h) for h in (0, 1) for o in lasts[1:]]
    table = np.zeros((2, 4, 8, 1, 256), np.int32)
    for core in (0, 1):
        for pair in range(8):
            sibling, first = divmod(pair, 4)
            offsets = []
            for last, half in own[2 * first : 2 * first + 2]:
                offsets += half_offsets(last, half)
            offsets = [mirrored(o) if core ^ sibling else o for o in offsets]
            table[core, :3, pair, 0] = np.repeat(np.array(offsets), 8, 0).T
            table[core, 3, pair, 0] = np.tile(np.arange(8), 32)
    return table


ORDER = order_constants()
VMEM = pl.BlockSpec(memory_space=pltpu.VMEM)
SMEM = pl.BlockSpec(memory_space=pltpu.SMEM)
ANY = pl.BlockSpec(memory_space=pl.ANY)
TOKEN = jax.ShapeDtypeStruct((8, 128), jnp.float32)


def near(x):
    return pltpu.with_memory_space_constraint(x, pltpu.VMEM)


def split_kernel(coupling_ref, source_ref, excite_ref, out_ref, token_ref, tiles, sems):
    token_ref[...] = jnp.zeros_like(token_ref)
    copies = []
    for tile in range(8):
        part = excite_ref.at[:, tile * 256 : tile * 256 + 256]
        copies.append(pltpu.make_async_copy(part, tiles.at[tile], sems.at[tile]))
        copies[-1].start()
    lane = lax.broadcasted_iota(jnp.int32, (256, 256), 0)
    goal = lax.broadcasted_iota(jnp.int32, (256, 256), 1)
    source = goal % 128 // 8 * 16 + goal // 128 * 8 + goal % 8
    move = (lane == source).astype(jnp.float32).astype(jnp.bfloat16)
    line = lax.broadcasted_iota(jnp.int32, (16, 256), 0)
    for tile in range(8):
        couple = coupling_ref[lax.axis_index("grp"), tile // 2]
        label = source_ref[:, tile * 256 : tile * 256 + 256] + tile // 2 * 64
        extra = jnp.where(line == 0, label, jnp.where(line == 1, couple, 0))
        copies[tile].wait()
        both = jnp.concatenate([tiles[tile], extra], 0).astype(jnp.float32).astype(jnp.bfloat16)
        moved = jnp.dot(both, move, preferred_element_type=jnp.float32).astype(jnp.bfloat16)
        out_ref[0, :, tile * 128 : tile * 128 + 128] = moved[:, :128]
        out_ref[1, :, tile * 128 : tile * 128 + 128] = moved[:, 128:]


def split_cores(coupling, source, excite):
    return pl.pallas_call(
        split_kernel,
        in_specs=[SMEM, VMEM, ANY],
        out_specs=[VMEM] * 2,
        out_shape=[pltpu.VMEM((2, 528, 1024), jnp.bfloat16), TOKEN],
        scratch_shapes=[pltpu.VMEM((8, 512, 256), jnp.int32), pltpu.SemaphoreType.DMA((8,))],
        compiler_params=pltpu.CompilerParams(vmem_limit_bytes=16 * MIB),
        cost_estimate=pl.CostEstimate(flops=2 * 528 * 2048 * 256, bytes_accessed=7 * MIB, transcendentals=0),
    )(coupling, source, pltpu.with_memory_space_constraint(excite, pltpu.HBM))


def arrange_kernel(order_ref, signs_ref, out_ref, token_ref):
    token_ref[...] = jnp.zeros_like(token_ref)
    blk, core = lax.axis_index("blk"), lax.axis_index("blk") % 2
    y, z, x = lax.axis_index("grp"), blk // 8, blk // 2 % 4

    @pl.loop(0, 8)
    def _(pair):
        dx, dy, dz, place = (jnp.where(core == 0, order_ref[0, i, pair], order_ref[1, i, pair]) for i in range(4))
        chip = (((y + dy) & 3) * NZ + ((z + dz) & 7)) * NX + ((x + dx) & 3)
        line = lax.broadcasted_iota(jnp.int32, (1024, 256), 0)
        move = (line == chip * 8 + place).astype(jnp.float32).astype(jnp.bfloat16)
        owner = jnp.where(pair < 4, core, 1 - core)
        moved = jnp.dot(signs_ref[owner], move, preferred_element_type=jnp.float32)
        out_ref[pair] = moved.astype(jnp.bfloat16)


def arrange(order, signs):
    return pl.pallas_call(
        arrange_kernel,
        in_specs=[VMEM] * 2,
        out_specs=[VMEM] * 2,
        out_shape=[pltpu.VMEM((8, 528, 256), jnp.bfloat16), TOKEN],
        compiler_params=pltpu.CompilerParams(vmem_limit_bytes=16 * MIB),
        cost_estimate=pl.CostEstimate(flops=2 * 528 * 2048 * 1024, bytes_accessed=4 * MIB, transcendentals=0),
    )(order, near(signs))


def lookup_kernel(target_ref, table_ref, signs_ref, out_ref, rows):
    labels = lax.broadcasted_iota(jnp.int32, (64, 512), 0)
    hot = (labels == target_ref[...]).astype(jnp.float32).astype(jnp.bfloat16)
    for part in range(2):
        table = jnp.concatenate([table_ref[:, 2 * h + part, :64] for h in range(4)], 1).astype(jnp.bfloat16)
        row = lax.dot_general(hot, table, (((0,), (0,)), ((), ())), preferred_element_type=jnp.float32)
        rows[part * 512 : part * 512 + 512, :] = row.astype(jnp.bfloat16)

    @pl.loop(0, 8)
    def _(pair):
        lines = lax.broadcasted_iota(jnp.int32, (256, 256), 0)
        extra = signs_ref[pair, 512:528, :].astype(jnp.float32)
        label = extra[0:1, :].astype(jnp.int32)
        pick = jnp.where(lines == label, extra[1:2, :], 0.0).astype(jnp.bfloat16)
        look = jnp.dot(rows[...], pick, preferred_element_type=jnp.float32)
        sign = signs_ref[pair, 0:512, :].astype(jnp.float32)
        for part in range(2):
            value = (look[part * 512 : part * 512 + 512] * sign).astype(jnp.bfloat16)
            for chunk in range(2):
                at = pl.multiple_of(pair * 512 + chunk * 256 + part * 128, 128)
                out_ref[:, pl.ds(at, 128)] = value[:, chunk * 128 : chunk * 128 + 128]


def lookup(target, table, signs):
    return pl.pallas_call(
        lookup_kernel,
        in_specs=[VMEM] * 3,
        out_specs=VMEM,
        out_shape=pltpu.VMEM((512, 4096), jnp.bfloat16),
        scratch_shapes=[pltpu.VMEM((1024, 256), jnp.bfloat16)],
        compiler_params=pltpu.CompilerParams(vmem_limit_bytes=16 * MIB),
        cost_estimate=pl.CostEstimate(flops=10**6, bytes_accessed=MIB, transcendentals=0),
    )(target, near(table), near(signs))


def join_kernel(groups, *refs):
    for group, out_ref in zip(groups, refs[len(refs) - len(groups) :]):
        pieces = [refs[k] for k in group]
        if pieces[0].shape[1] % 16:
            out_ref[...] = jnp.concatenate([piece[...] for piece in pieces], 1)
            continue
        at = 0
        for piece in pieces:
            out_ref[:, at : at + piece.shape[1], :] = piece[...]
            at += piece.shape[1]


def join(pieces, groups, after=()):
    shapes = [(2, sum(pieces[k].shape[1] for k in group), 1024) for group in groups]
    return pl.pallas_call(
        functools.partial(join_kernel, groups),
        in_specs=[VMEM] * len(pieces) + [ANY] * len(after),
        out_specs=[VMEM] * len(groups),
        out_shape=[pltpu.VMEM(shape, jnp.bfloat16) for shape in shapes],
        compiler_params=pltpu.CompilerParams(vmem_limit_bytes=8 * MIB),
        cost_estimate=pl.CostEstimate(flops=0, bytes_accessed=MIB, transcendentals=0),
    )(*[near(p) for p in pieces], *after)


def product_kernel(first, last, starts, count, width, *refs):
    live_ref, left_ref = refs[:2]
    blocks = refs[2 : 2 + count]
    total_ref = None if first else refs[2 + count]
    out_ref, right = refs[-2 - (not last)], refs[-1]
    pieces = [(block, row) for block in blocks for row in range(0, block.shape[1], 128)]
    if not last:
        refs[-2][...] = jnp.zeros_like(refs[-2])

    def columns(n):
        at = pl.ds(pl.multiple_of(n * width, width), width)
        for part in range(2):
            for k, (block, row) in enumerate(pieces):
                right[k * 256 : k * 256 + 128, :] = block[part, row : row + 128, at]
                other = block[1 - part, row : row + 128, at]
                right[k * 256 + 128 : k * 256 + 256, :] = other if part else -other
            acc = None if first else total_ref[part, :, at]
            row = 0
            for start, deep in starts:
                left = left_ref[:, start : start + deep]
                more = jnp.dot(left, right[row : row + deep, :], preferred_element_type=jnp.float32)
                acc = more if acc is None else acc + more
                row += deep
            if last:
                line = lax.broadcasted_iota(jnp.int32, acc.shape, 0)
                out_ref[part] = jnp.where(line < live_ref[0], acc, 0.0)
            else:
                out_ref[part, :, at] = acc

    if last:
        columns(pl.program_id(0))
    else:
        pl.loop(0, 1024 // width)(columns)


def product(live, left, starts, blocks, total, last, flops=10**6, width=512):
    count = len(blocks)
    first = total is None
    arrays = [near(a) for a in [left, *blocks] + ([] if first else [total])]
    shape = (2, 512, 1024)
    if last:
        out = dict(
            grid=(1024 // width,),
            out_specs=pl.BlockSpec((2, 512, width), lambda n: (0, 0, n)),
            out_shape=jax.ShapeDtypeStruct(shape, jnp.float32),
        )
    else:
        out = dict(
            out_specs=[VMEM] * 2,
            out_shape=[pltpu.VMEM(shape, jnp.float32), TOKEN],
        )
        if not first:
            out["input_output_aliases"] = {2 + count: 0}
    deep = sum(2 * b.shape[1] for b in blocks)
    return pl.pallas_call(
        functools.partial(product_kernel, first, last, starts, count, width),
        in_specs=[SMEM] + [VMEM] * len(arrays),
        scratch_shapes=[pltpu.VMEM((deep, width), jnp.bfloat16)],
        compiler_params=pltpu.CompilerParams(vmem_limit_bytes=16 * MIB),
        cost_estimate=pl.CostEstimate(flops=flops, bytes_accessed=MIB, transcendentals=0),
        **out,
    )(live, *arrays)


def spread_kernel(row_ref, after_ref, out_ref):
    del after_ref
    row = row_ref[...]
    row = jnp.concatenate([row, jnp.zeros_like(row)], 1)
    out_ref[...] = jnp.broadcast_to(row[None], out_ref.shape)


def spread(row, after):
    return pl.pallas_call(
        spread_kernel,
        in_specs=[VMEM] * 2,
        out_specs=VMEM,
        out_shape=jax.ShapeDtypeStruct((64, 8, 128), jnp.float32),
        cost_estimate=pl.CostEstimate(flops=10**6, bytes_accessed=MIB, transcendentals=0),
    )(row, near(after))


def on_device(coeffs, coupling, one_body, target_orb, source_orb, excite, live_rows):
    signs, token = split_cores(coupling, source_orb[None, :], excite)
    slab = join([coeffs] + fetch(coeffs, 0), [(0, 1)], [token])[0]

    table = lax.all_to_all(spread(one_body.reshape(8, 64), slab), "blk", 0, 0, tiled=True)

    slab = join([slab] + fetch(slab, 1), [(0, 1, 2, 3)], [table])[0]
    arranged, token = arrange(ORDER, signs)
    halves = list(join([slab] + fetch(slab, 2), [(0, 1), (2, 3)], [token]))
    left = lookup(target_orb[None, :], table, arranged)

    got = [fetch(half, 3) for half in halves]
    own = halves + [swap(half) for half in halves]
    total, token = product(live_rows, left, ((0, 512), (2048, 512)), own, None, False)
    first = join(got[0], [(0, 1, 2)], [token])[0]
    their_first = swap(first)
    total, token = product(live_rows, left, ((512, 768),), [first], total, False)
    second = join(got[1], [(0, 1, 2)], [token])[0]
    their_second = swap(second)
    total, _ = product(live_rows, left, ((2560, 768), (1280, 768)), [their_first, second], total, False)
    return product(live_rows, left, ((3328, 768),), [their_second], total, True)


def solution(mesh):
    from jax.sharding import PartitionSpec as P

    return jax.shard_map(
        on_device,
        mesh=mesh,
        in_specs=(
            P(None, ("grp", "blk"), None),
            P(),
            P("grp", None, None, "blk", None),
            P(("grp", "blk")),
            P(),
            P(("grp", "blk"), None),
            P(("grp", "blk")),
        ),
        out_specs=P(None, ("grp", "blk"), None),
        check_vma=False,
    )
```

```python
import functools

import jax
import jax.numpy as jnp
import numpy as np
from jax import lax
from jax.experimental import pallas as pl
from jax.experimental.pallas import tpu as pltpu

NY, NZ, NX = 4, 8, 4
AXES = ("grp", "blk")
STAGES = (
    ((0, 0, 4),),
    ((2, 0, 1), (0, 0, 2), (2, 0, -1)),
    ((0, 1, 1), (0, 2, 0), (0, -1, 1)),
    ((1, 0, 0), (-1, 0, 0), (0, 0, 1)),
)
HERE = ((0, 0, 0),)
SWAP = [(i, i ^ 1) for i in range(NY * NZ * NX * 2)]
MIB = 1 << 20


def mirrored(o):
    return (o[1], o[0], -o[2])


def index(x, y, z, c):
    return ((y % NY * NZ + z % NZ) * NX + x % NX) * 2 + c


def route(offset):
    pairs = []
    for y in range(NY):
        for z in range(NZ):
            for x in range(NX):
                for c in range(2):
                    dx, dy, dz = mirrored(offset) if c else offset
                    pairs.append((index(x + dx, y + dy, z + dz, c), index(x, y, z, c)))
    return pairs


def fetch(block, stage):
    return [lax.ppermute(block, AXES, route(o)) for o in STAGES[stage]]


def swap(block):
    return lax.ppermute(block, AXES, SWAP)


def half_offsets(last, half):
    second = HERE + STAGES[2]
    out = []
    for o2 in second[2 * half : 2 * half + 2]:
        for o1 in HERE + STAGES[1]:
            for o0 in HERE + STAGES[0]:
                out.append([sum(t) for t in zip(last, o2, o1, o0)])
    return out


def order_constants():
    lasts = HERE + STAGES[3]
    own = [(lasts[0], 0), (lasts[0], 1)] + [(o, h) for h in (0, 1) for o in lasts[1:]]
    table = np.zeros((2, 4, 8, 1, 256), np.int32)
    for core in (0, 1):
        for pair in range(8):
            sibling, first = divmod(pair, 4)
            offsets = []
            for last, half in own[2 * first : 2 * first + 2]:
                offsets += half_offsets(last, half)
            offsets = [mirrored(o) if core ^ sibling else o for o in offsets]
            table[core, :3, pair, 0] = np.repeat(np.array(offsets), 8, 0).T
            table[core, 3, pair, 0] = np.tile(np.arange(8), 32)
    return table


ORDER = order_constants()
VMEM = pl.BlockSpec(memory_space=pltpu.VMEM)
SMEM = pl.BlockSpec(memory_space=pltpu.SMEM)
ANY = pl.BlockSpec(memory_space=pl.ANY)
TOKEN = jax.ShapeDtypeStruct((8, 128), jnp.float32)


def near(x):
    return pltpu.with_memory_space_constraint(x, pltpu.VMEM)


def split_kernel(coupling_ref, source_ref, excite_ref, out_ref, token_ref, tiles, labels, couples, sems):
    token_ref[...] = jnp.zeros_like(token_ref)
    small = [
        pltpu.make_async_copy(coupling_ref, couples, sems.at[8]),
        pltpu.make_async_copy(source_ref, labels, sems.at[9]),
    ]
    for copy in small:
        copy.start()
    copies = []
    for tile in range(8):
        part = excite_ref.at[:, tile * 256 : tile * 256 + 256]
        copies.append(pltpu.make_async_copy(part, tiles.at[tile], sems.at[tile]))
        copies[-1].start()
    lane = lax.broadcasted_iota(jnp.int32, (256, 256), 0)
    goal = lax.broadcasted_iota(jnp.int32, (256, 256), 1)
    source = goal % 128 // 8 * 16 + goal // 128 * 8 + goal % 8
    move = (lane == source).astype(jnp.float32).astype(jnp.bfloat16)
    line = lax.broadcasted_iota(jnp.int32, (16, 256), 0)
    for copy in small:
        copy.wait()
    for tile in range(8):
        couple = couples[lax.axis_index("grp"), tile // 2]
        label = labels[:, tile * 256 : tile * 256 + 256] + tile // 2 * 64
        extra = jnp.where(line == 0, label, jnp.where(line == 1, couple, 0))
        copies[tile].wait()
        both = jnp.concatenate([tiles[tile], extra], 0).astype(jnp.float32).astype(jnp.bfloat16)
        moved = jnp.dot(both, move, preferred_element_type=jnp.float32).astype(jnp.bfloat16)
        out_ref[0, :, tile * 128 : tile * 128 + 128] = moved[:, :128]
        out_ref[1, :, tile * 128 : tile * 128 + 128] = moved[:, 128:]


def split_cores(coupling, source, excite):
    return pl.pallas_call(
        split_kernel,
        in_specs=[ANY] * 3,
        out_specs=[VMEM] * 2,
        out_shape=[pltpu.VMEM((2, 528, 1024), jnp.bfloat16), TOKEN],
        scratch_shapes=[
            pltpu.VMEM((8, 512, 256), jnp.int32),
            pltpu.VMEM((1, 2048), jnp.int32),
            pltpu.SMEM((4, 4), jnp.int32),
            pltpu.SemaphoreType.DMA((10,)),
        ],
        compiler_params=pltpu.CompilerParams(vmem_limit_bytes=16 * MIB),
        cost_estimate=pl.CostEstimate(flops=2 * 528 * 2048 * 256, bytes_accessed=7 * MIB, transcendentals=0),
    )(*[pltpu.with_memory_space_constraint(a, pltpu.HBM) for a in (coupling, source, excite)])


def arrange_kernel(order_ref, signs_ref, out_ref, token_ref):
    token_ref[...] = jnp.zeros_like(token_ref)
    blk, core = lax.axis_index("blk"), lax.axis_index("blk") % 2
    y, z, x = lax.axis_index("grp"), blk // 8, blk // 2 % 4

    @pl.loop(0, 8)
    def _(pair):
        dx, dy, dz, place = (jnp.where(core == 0, order_ref[0, i, pair], order_ref[1, i, pair]) for i in range(4))
        chip = (((y + dy) & 3) * NZ + ((z + dz) & 7)) * NX + ((x + dx) & 3)
        line = lax.broadcasted_iota(jnp.int32, (1024, 256), 0)
        move = (line == chip * 8 + place).astype(jnp.float32).astype(jnp.bfloat16)
        owner = jnp.where(pair < 4, core, 1 - core)
        moved = jnp.dot(signs_ref[owner], move, preferred_element_type=jnp.float32)
        out_ref[pair] = moved.astype(jnp.bfloat16)


def arrange(order, signs):
    return pl.pallas_call(
        arrange_kernel,
        in_specs=[VMEM] * 2,
        out_specs=[VMEM] * 2,
        out_shape=[pltpu.VMEM((8, 528, 256), jnp.bfloat16), TOKEN],
        compiler_params=pltpu.CompilerParams(vmem_limit_bytes=16 * MIB),
        cost_estimate=pl.CostEstimate(flops=2 * 528 * 2048 * 1024, bytes_accessed=4 * MIB, transcendentals=0),
    )(order, near(signs))


def table_labels(shape):
    blk = lax.axis_index("blk")
    core, z, x = blk % 2, blk // 8, blk // 2 % 4
    row = lax.broadcasted_iota(jnp.int32, shape, 0)
    along, owner, chip = row >> 4, (row >> 3) & 1, row & 7
    side = 1 + 2 * core
    dx = jnp.where(along == 1, side, jnp.where(along == 2, 4 - side, jnp.where(along == 3, 2, 0)))
    second, first = chip >> 1, chip & 1
    dx = dx + 2 * (second & 1)
    dz = 4 * first + jnp.where(second == 3, 7, second)
    return ((z + dz) & 7) * 8 + ((x + dx) & 3) * 2 + owner


def lookup_kernel(target_ref, signs_ref, after_ref, *refs):
    del after_ref
    tables, (out_ref, token_ref, rows) = refs[:4], refs[4:]
    token_ref[...] = jnp.zeros_like(token_ref)
    hot = (table_labels((64, 512)) == target_ref[...]).astype(jnp.float32).astype(jnp.bfloat16)
    entries = [ref[...].reshape(8, 8, 128) for ref in tables]
    for part in range(2):
        lines = [
            jnp.concatenate([entry[:, 2 * h + part, core * 64 : core * 64 + 64] for h in range(4)], 1)
            for entry in entries
            for core in range(2)
        ]
        table = jnp.concatenate(lines, 0).astype(jnp.bfloat16)
        row = lax.dot_general(hot, table, (((0,), (0,)), ((), ())), preferred_element_type=jnp.float32)
        rows[part * 512 : part * 512 + 512, :] = row.astype(jnp.bfloat16)

    @pl.loop(0, 8)
    def _(pair):
        lines = lax.broadcasted_iota(jnp.int32, (256, 256), 0)
        extra = signs_ref[pair, 512:528, :].astype(jnp.float32)
        label = extra[0:1, :].astype(jnp.int32)
        pick = jnp.where(lines == label, extra[1:2, :], 0.0).astype(jnp.bfloat16)
        look = jnp.dot(rows[...], pick, preferred_element_type=jnp.float32)
        sign = signs_ref[pair, 0:512, :].astype(jnp.float32)
        for part in range(2):
            value = (look[part * 512 : part * 512 + 512] * sign).astype(jnp.bfloat16)
            for chunk in range(2):
                at = pl.multiple_of(pair * 512 + chunk * 256 + part * 128, 128)
                out_ref[:, pl.ds(at, 128)] = value[:, chunk * 128 : chunk * 128 + 128]


def lookup(target, tables, signs, after):
    return pl.pallas_call(
        lookup_kernel,
        in_specs=[VMEM] * 7,
        out_specs=[VMEM] * 2,
        out_shape=[pltpu.VMEM((512, 4096), jnp.bfloat16), TOKEN],
        scratch_shapes=[pltpu.VMEM((1024, 256), jnp.bfloat16)],
        compiler_params=pltpu.CompilerParams(vmem_limit_bytes=16 * MIB),
        cost_estimate=pl.CostEstimate(flops=10**6, bytes_accessed=MIB, transcendentals=0),
    )(target, *[near(a) for a in (signs, after, *tables)])


def join_kernel(groups, *refs):
    for group, out_ref in zip(groups, refs[len(refs) - len(groups) :]):
        pieces = [refs[k] for k in group]
        if pieces[0].shape[1] % 16:
            out_ref[...] = jnp.concatenate([piece[...] for piece in pieces], 1)
            continue
        at = 0
        for piece in pieces:
            out_ref[:, at : at + piece.shape[1], :] = piece[...]
            at += piece.shape[1]


def join(pieces, groups, after=()):
    shapes = [(2, sum(pieces[k].shape[1] for k in group), pieces[0].shape[2]) for group in groups]
    return pl.pallas_call(
        functools.partial(join_kernel, groups),
        in_specs=[VMEM] * (len(pieces) + len(after)),
        out_specs=[VMEM] * len(groups),
        out_shape=[pltpu.VMEM(shape, jnp.bfloat16) for shape in shapes],
        compiler_params=pltpu.CompilerParams(vmem_limit_bytes=4 * MIB),
        cost_estimate=pl.CostEstimate(flops=0, bytes_accessed=MIB, transcendentals=0),
    )(*[near(p) for p in pieces], *after)


def relay_kernel(block_ref, after_ref, out_ref):
    del block_ref, after_ref, out_ref


def relay(block, after):
    return pl.pallas_call(
        relay_kernel,
        in_specs=[VMEM] * 2,
        out_specs=VMEM,
        out_shape=pltpu.VMEM(block.shape, block.dtype),
        input_output_aliases={0: 0},
        compiler_params=pltpu.CompilerParams(vmem_limit_bytes=2 * MIB),
        cost_estimate=pl.CostEstimate(flops=0, bytes_accessed=0, transcendentals=0),
    )(near(block), after)


def product_kernel(first, last, starts, count, width, *refs):
    live_ref, left_ref = refs[:2]
    blocks = refs[2 : 2 + count]
    total_ref = None if first else refs[2 + count]
    out_ref, right = refs[-2 - (not last)], refs[-1]
    pieces = [(block, row) for block in blocks for row in range(0, block.shape[1], 128)]
    if not last:
        refs[-2][...] = jnp.zeros_like(refs[-2])

    def columns(n):
        at = pl.ds(pl.multiple_of(n * width, width), width)
        for part in range(2):
            for k, (block, row) in enumerate(pieces):
                right[k * 256 : k * 256 + 128, :] = block[part, row : row + 128, at]
                other = block[1 - part, row : row + 128, at]
                right[k * 256 + 128 : k * 256 + 256, :] = other if part else -other
            acc = None if first else total_ref[part, :, at]
            row = 0
            for start, deep in starts:
                left = left_ref[:, start : start + deep]
                more = jnp.dot(left, right[row : row + deep, :], preferred_element_type=jnp.float32)
                acc = more if acc is None else acc + more
                row += deep
            if last:
                line = lax.broadcasted_iota(jnp.int32, acc.shape, 0)
                out_ref[part] = jnp.where(line < live_ref[0], acc, 0.0)
            else:
                out_ref[part, :, at] = acc

    if last:
        columns(pl.program_id(0))
    else:
        pl.loop(0, 1024 // width)(columns)


def product(live, left, starts, blocks, total, last, flops=10**6, width=512):
    count = len(blocks)
    first = total is None
    arrays = [near(a) for a in [left, *blocks] + ([] if first else [total])]
    shape = (2, 512, 1024)
    if last:
        out = dict(
            grid=(1024 // width,),
            out_specs=pl.BlockSpec((2, 512, width), lambda n: (0, 0, n)),
            out_shape=jax.ShapeDtypeStruct(shape, jnp.float32),
        )
    else:
        out = dict(
            out_specs=[VMEM] * 2,
            out_shape=[pltpu.VMEM(shape, jnp.float32), TOKEN],
        )
        if not first:
            out["input_output_aliases"] = {2 + count: 0}
    deep = sum(2 * b.shape[1] for b in blocks)
    return pl.pallas_call(
        functools.partial(product_kernel, first, last, starts, count, width),
        in_specs=[SMEM] + [VMEM] * len(arrays),
        scratch_shapes=[pltpu.VMEM((deep, width), jnp.bfloat16)],
        compiler_params=pltpu.CompilerParams(vmem_limit_bytes=16 * MIB),
        cost_estimate=pl.CostEstimate(flops=flops, bytes_accessed=MIB, transcendentals=0),
        **out,
    )(live, *arrays)


def along_x(first, second):
    pairs = []
    for y in range(NY):
        for z in range(NZ):
            for x in range(NX):
                for c, step in enumerate((first, second)):
                    pairs.append((index(x + step, y, z, c), index(x, y, z, c)))
    return pairs


def choose(mine, theirs):
    return jnp.where(lax.axis_index("blk") % 2 == 0, mine, theirs)


def pack_kernel(coeffs_ref, mine_ref, theirs_ref, out_ref):
    mine, theirs = mine_ref[...], theirs_ref[...]
    entries = jnp.concatenate([choose(mine, theirs), choose(theirs, mine)], 1).astype(jnp.bfloat16)
    out_ref[:, :, :1024] = coeffs_ref[...]
    out_ref[0, :, 1024:] = entries
    out_ref[1, :, 1024:] = jnp.zeros_like(entries)


def pack(coeffs, mine, theirs):
    return pl.pallas_call(
        pack_kernel,
        in_specs=[VMEM] * 3,
        out_specs=VMEM,
        out_shape=pltpu.VMEM((2, 8, 1152), jnp.bfloat16),
        compiler_params=pltpu.CompilerParams(vmem_limit_bytes=2 * MIB),
        cost_estimate=pl.CostEstimate(flops=0, bytes_accessed=1 << 16, transcendentals=0),
    )(coeffs, mine, theirs)


def unpack_kernel(*refs):
    pieces, slab_ref, table_ref = refs[:4], refs[-2], refs[-1]
    for k, piece in enumerate(pieces):
        slab_ref[:, k * 16 : k * 16 + 16, :] = piece[:, :, :1024]
        table_ref[k * 16 : k * 16 + 16, :] = piece[0, :, 1024:].astype(jnp.float32)


def unpack(pieces, after):
    return pl.pallas_call(
        unpack_kernel,
        in_specs=[VMEM] * 4 + [ANY],
        out_specs=[VMEM] * 2,
        out_shape=[pltpu.VMEM((2, 64, 1024), jnp.bfloat16), pltpu.VMEM((64, 128), jnp.float32)],
        compiler_params=pltpu.CompilerParams(vmem_limit_bytes=2 * MIB),
        cost_estimate=pl.CostEstimate(flops=0, bytes_accessed=MIB, transcendentals=0),
    )(*[near(piece) for piece in pieces], after)


def pick_kernel(mine_ref, theirs_ref, out_ref):
    out_ref[...] = choose(mine_ref[...], theirs_ref[...])


def pick(mine, theirs):
    return pl.pallas_call(
        pick_kernel,
        in_specs=[VMEM] * 2,
        out_specs=VMEM,
        out_shape=pltpu.VMEM((64, 128), jnp.float32),
        compiler_params=pltpu.CompilerParams(vmem_limit_bytes=2 * MIB),
        cost_estimate=pl.CostEstimate(flops=0, bytes_accessed=1 << 16, transcendentals=0),
    )(near(mine), near(theirs))


def gather_tables(table):
    table = pick(table, swap(table))
    side = lax.ppermute(table, AXES, along_x(1, -1))
    return [table, side, swap(side), lax.ppermute(table, AXES, along_x(2, 2))]


def on_device(coeffs, coupling, one_body, target_orb, source_orb, excite, live_rows):
    signs, token = split_cores(coupling, source_orb[None, :], excite)
    row = one_body.reshape(8, 64)
    packed = pack(coeffs, row, swap(row))
    packed = join([packed] + fetch(packed, 0), [(0, 1)], [token])[0]
    arranged, token = arrange(ORDER, signs)
    slab, table = unpack([packed] + fetch(packed, 1), token)
    tables = gather_tables(table)
    halves = list(
        join([slab] + fetch(slab, 2), [(0, 1), (2, 3), (2, 3)], [near(tables[1]), near(tables[3])])
    )
    spare = halves.pop()
    left, token = lookup(target_orb[None, :], tables, arranged, halves[0])
    late = relay(spare, token)

    got = [fetch(halves[0], 3)]
    got.append([lax.ppermute(h, AXES, route(o)) for h, o in zip((halves[1], halves[1], late), STAGES[3])])
    own = halves + [swap(half) for half in halves]
    total, token = product(live_rows, left, ((0, 512), (2048, 512)), own, None, False)
    first = join(got[0], [(0, 1, 2)], [token])[0]
    their_first = swap(first)
    total, token = product(live_rows, left, ((512, 768),), [first], total, False)
    second = join(got[1], [(0, 1, 2)], [token])[0]
    their_second = swap(second)
    total, _ = product(live_rows, left, ((2560, 768), (1280, 768)), [their_first, second], total, False)
    return product(live_rows, left, ((3328, 768),), [their_second], total, True)


def solution(mesh):
    from jax.sharding import PartitionSpec as P

    return jax.shard_map(
        on_device,
        mesh=mesh,
        in_specs=(
            P(None, ("grp", "blk"), None),
            P(),
            P("grp", None, None, "blk", None),
            P(("grp", "blk")),
            P(),
            P(("grp", "blk"), None),
            P(("grp", "blk")),
        ),
        out_specs=P(None, ("grp", "blk"), None),
        check_vma=False,
    )
```

```python
import functools

import jax
import jax.numpy as jnp
import numpy as np
from jax import lax
from jax.experimental import pallas as pl
from jax.experimental.pallas import tpu as pltpu

NY, NZ, NX = 4, 8, 4
AXES = ("grp", "blk")
STAGES = (
    ((0, 0, 4),),
    ((2, 0, 1), (0, 0, 2), (2, 0, -1)),
    ((0, 1, 1), (0, 2, 0), (0, -1, 1)),
    ((1, 0, 0), (-1, 0, 0), (0, 0, 1)),
)
HERE = ((0, 0, 0),)
SWAP = [(i, i ^ 1) for i in range(NY * NZ * NX * 2)]
MIB = 1 << 20


def mirrored(o):
    return (o[1], o[0], -o[2])


def index(x, y, z, c):
    return ((y % NY * NZ + z % NZ) * NX + x % NX) * 2 + c


def route(offset):
    pairs = []
    for y in range(NY):
        for z in range(NZ):
            for x in range(NX):
                for c in range(2):
                    dx, dy, dz = mirrored(offset) if c else offset
                    pairs.append((index(x + dx, y + dy, z + dz, c), index(x, y, z, c)))
    return pairs


def fetch(block, stage):
    return [lax.ppermute(block, AXES, route(o)) for o in STAGES[stage]]


def swap(block):
    return lax.ppermute(block, AXES, SWAP)


def half_offsets(last, half):
    second = HERE + STAGES[2]
    out = []
    for o2 in second[2 * half : 2 * half + 2]:
        for o1 in HERE + STAGES[1]:
            for o0 in HERE + STAGES[0]:
                out.append([sum(t) for t in zip(last, o2, o1, o0)])
    return out


def order_constants():
    lasts = HERE + STAGES[3]
    own = [(lasts[0], 0), (lasts[0], 1)] + [(o, h) for h in (0, 1) for o in lasts[1:]]
    table = np.zeros((2, 4, 8, 1, 256), np.int32)
    for core in (0, 1):
        for pair in range(8):
            sibling, first = divmod(pair, 4)
            offsets = []
            for last, half in own[2 * first : 2 * first + 2]:
                offsets += half_offsets(last, half)
            offsets = [mirrored(o) if core ^ sibling else o for o in offsets]
            table[core, :3, pair, 0] = np.repeat(np.array(offsets), 8, 0).T
            table[core, 3, pair, 0] = np.tile(np.arange(8), 32)
    return table


ORDER = order_constants()
VMEM = pl.BlockSpec(memory_space=pltpu.VMEM)
SMEM = pl.BlockSpec(memory_space=pltpu.SMEM)
ANY = pl.BlockSpec(memory_space=pl.ANY)
TOKEN = jax.ShapeDtypeStruct((8, 128), jnp.float32)


def near(x):
    return pltpu.with_memory_space_constraint(x, pltpu.VMEM)


def split_kernel(coupling_ref, source_ref, excite_ref, out_ref, token_ref, tiles, labels, couples, sems):
    token_ref[...] = jnp.zeros_like(token_ref)
    small = [
        pltpu.make_async_copy(coupling_ref, couples, sems.at[8]),
        pltpu.make_async_copy(source_ref, labels, sems.at[9]),
    ]
    for copy in small:
        copy.start()
    copies = []
    for tile in range(8):
        part = excite_ref.at[:, tile * 256 : tile * 256 + 256]
        copies.append(pltpu.make_async_copy(part, tiles.at[tile], sems.at[tile]))
        copies[-1].start()
    lane = lax.broadcasted_iota(jnp.int32, (256, 256), 0)
    goal = lax.broadcasted_iota(jnp.int32, (256, 256), 1)
    source = goal % 128 // 8 * 16 + goal // 128 * 8 + goal % 8
    move = (lane == source).astype(jnp.float32).astype(jnp.bfloat16)
    line = lax.broadcasted_iota(jnp.int32, (16, 256), 0)
    for copy in small:
        copy.wait()
    for tile in range(8):
        couple = couples[lax.axis_index("grp"), tile // 2]
        label = labels[:, tile * 256 : tile * 256 + 256] + tile // 2 * 64
        extra = jnp.where(line == 0, label, jnp.where(line == 1, couple, 0))
        copies[tile].wait()
        both = jnp.concatenate([tiles[tile], extra], 0).astype(jnp.float32).astype(jnp.bfloat16)
        moved = jnp.dot(both, move, preferred_element_type=jnp.float32).astype(jnp.bfloat16)
        out_ref[0, :, tile * 128 : tile * 128 + 128] = moved[:, :128]
        out_ref[1, :, tile * 128 : tile * 128 + 128] = moved[:, 128:]


def split_cores(coupling, source, excite):
    return pl.pallas_call(
        split_kernel,
        in_specs=[ANY] * 3,
        out_specs=[VMEM] * 2,
        out_shape=[pltpu.VMEM((2, 528, 1024), jnp.bfloat16), TOKEN],
        scratch_shapes=[
            pltpu.VMEM((8, 512, 256), jnp.int32),
            pltpu.VMEM((1, 2048), jnp.int32),
            pltpu.SMEM((4, 4), jnp.int32),
            pltpu.SemaphoreType.DMA((10,)),
        ],
        compiler_params=pltpu.CompilerParams(vmem_limit_bytes=16 * MIB),
        cost_estimate=pl.CostEstimate(flops=2 * 528 * 2048 * 256, bytes_accessed=7 * MIB, transcendentals=0),
    )(*[pltpu.with_memory_space_constraint(a, pltpu.HBM) for a in (coupling, source, excite)])


def arrange_kernel(order_ref, signs_ref, out_ref, token_ref):
    token_ref[...] = jnp.zeros_like(token_ref)
    blk, core = lax.axis_index("blk"), lax.axis_index("blk") % 2
    y, z, x = lax.axis_index("grp"), blk // 8, blk // 2 % 4

    @pl.loop(0, 8)
    def _(pair):
        dx, dy, dz, place = (jnp.where(core == 0, order_ref[0, i, pair], order_ref[1, i, pair]) for i in range(4))
        chip = (((y + dy) & 3) * NZ + ((z + dz) & 7)) * NX + ((x + dx) & 3)
        line = lax.broadcasted_iota(jnp.int32, (1024, 256), 0)
        move = (line == chip * 8 + place).astype(jnp.float32).astype(jnp.bfloat16)
        owner = jnp.where(pair < 4, core, 1 - core)
        moved = jnp.dot(signs_ref[owner], move, preferred_element_type=jnp.float32)
        out_ref[pair] = moved.astype(jnp.bfloat16)


def arrange(order, signs):
    return pl.pallas_call(
        arrange_kernel,
        in_specs=[VMEM] * 2,
        out_specs=[VMEM] * 2,
        out_shape=[pltpu.VMEM((8, 528, 256), jnp.bfloat16), TOKEN],
        compiler_params=pltpu.CompilerParams(vmem_limit_bytes=16 * MIB),
        cost_estimate=pl.CostEstimate(flops=2 * 528 * 2048 * 1024, bytes_accessed=4 * MIB, transcendentals=0),
    )(order, near(signs))


def table_labels(shape):
    blk = lax.axis_index("blk")
    core, z, x = blk % 2, blk // 8, blk // 2 % 4
    row = lax.broadcasted_iota(jnp.int32, shape, 0)
    along, owner, chip = row >> 4, (row >> 3) & 1, row & 7
    side = 1 + 2 * core
    dx = jnp.where(along == 1, side, jnp.where(along == 2, 4 - side, jnp.where(along == 3, 2, 0)))
    second, first = chip >> 1, chip & 1
    dx = dx + 2 * (second & 1)
    dz = 4 * first + jnp.where(second == 3, 7, second)
    return ((z + dz) & 7) * 8 + ((x + dx) & 3) * 2 + owner


def lookup_kernel(target_ref, signs_ref, after_ref, *refs):
    del after_ref
    tables, (out_ref, token_ref, rows) = refs[:4], refs[4:]
    token_ref[...] = jnp.zeros_like(token_ref)
    hot = (table_labels((64, 512)) == target_ref[...]).astype(jnp.float32).astype(jnp.bfloat16)
    entries = [ref[...].reshape(8, 8, 128) for ref in tables]
    for part in range(2):
        lines = [
            jnp.concatenate([entry[:, 2 * h + part, core * 64 : core * 64 + 64] for h in range(4)], 1)
            for entry in entries
            for core in range(2)
        ]
        table = jnp.concatenate(lines, 0).astype(jnp.bfloat16)
        row = lax.dot_general(hot, table, (((0,), (0,)), ((), ())), preferred_element_type=jnp.float32)
        rows[part * 512 : part * 512 + 512, :] = row.astype(jnp.bfloat16)

    for pair in range(8):
        lines = lax.broadcasted_iota(jnp.int32, (256, 256), 0)
        extra = signs_ref[pair, 512:528, :].astype(jnp.float32)
        label = extra[0:1, :].astype(jnp.int32)
        choice = jnp.where(lines == label, extra[1:2, :], 0.0).astype(jnp.bfloat16)
        look = jnp.dot(rows[...], choice, preferred_element_type=jnp.float32).astype(jnp.bfloat16)
        sign = signs_ref[pair, 0:512, :]
        real, imag = look[:512] * sign, look[512:] * sign
        for half in range(2):
            at, step = column(2 * pair + half)
            piece = slice(half * 128, half * 128 + 128)
            out_ref[:512, at : at + 128] = real[:, piece]
            out_ref[:512, at + step : at + step + 128] = -imag[:, piece]
            out_ref[512:, at : at + 128] = imag[:, piece]
            out_ref[512:, at + step : at + step + 128] = real[:, piece]


def column(chunk):
    sibling, chunk = divmod(chunk, 8)
    if chunk < 2:
        return sibling * 2048 + chunk * 256, 128
    group, place = divmod(chunk - 2, 3)
    return sibling * 2048 + 512 + group * 768 + place * 128, 384


def lookup(target, tables, signs, after):
    return pl.pallas_call(
        lookup_kernel,
        in_specs=[VMEM] * 7,
        out_specs=[VMEM] * 2,
        out_shape=[pltpu.VMEM((1024, 4096), jnp.bfloat16), TOKEN],
        scratch_shapes=[pltpu.VMEM((1024, 256), jnp.bfloat16)],
        compiler_params=pltpu.CompilerParams(vmem_limit_bytes=16 * MIB),
        cost_estimate=pl.CostEstimate(flops=10**6, bytes_accessed=MIB, transcendentals=0),
    )(target, *[near(a) for a in (signs, after, *tables)])


def join_kernel(groups, *refs):
    for group, out_ref in zip(groups, refs[len(refs) - len(groups) :]):
        pieces = [refs[k] for k in group]
        if pieces[0].shape[1] % 16:
            out_ref[...] = jnp.concatenate([piece[...] for piece in pieces], 1)
            continue
        at = 0
        for piece in pieces:
            out_ref[:, at : at + piece.shape[1], :] = piece[...]
            at += piece.shape[1]


def join(pieces, groups, after=()):
    shapes = [(2, sum(pieces[k].shape[1] for k in group), pieces[0].shape[2]) for group in groups]
    return pl.pallas_call(
        functools.partial(join_kernel, groups),
        in_specs=[VMEM] * (len(pieces) + len(after)),
        out_specs=[VMEM] * len(groups),
        out_shape=[pltpu.VMEM(shape, jnp.bfloat16) for shape in shapes],
        compiler_params=pltpu.CompilerParams(vmem_limit_bytes=4 * MIB),
        cost_estimate=pl.CostEstimate(flops=0, bytes_accessed=MIB, transcendentals=0),
    )(*[near(p) for p in pieces], *after)


def relay_kernel(block_ref, after_ref, out_ref):
    del block_ref, after_ref, out_ref


def relay(block, after):
    return pl.pallas_call(
        relay_kernel,
        in_specs=[VMEM] * 2,
        out_specs=VMEM,
        out_shape=pltpu.VMEM(block.shape, block.dtype),
        input_output_aliases={0: 0},
        compiler_params=pltpu.CompilerParams(vmem_limit_bytes=2 * MIB),
        cost_estimate=pl.CostEstimate(flops=0, bytes_accessed=0, transcendentals=0),
    )(near(block), after)


def product_kernel(first, last, starts, width, *refs):
    live_ref, left_ref = refs[:2]
    blocks = refs[2 : 2 + len(starts)]
    total_ref = None if first else refs[2 + len(starts)]
    out_ref = refs[-1 - (not last)]
    if not last:
        refs[-1][...] = jnp.zeros_like(refs[-1])

    def columns(n):
        at = pl.ds(pl.multiple_of(n * width, width), width)
        acc = None if first else total_ref[:, :, at].reshape(1024, width)
        for start, block in zip(starts, blocks):
            deep = 2 * block.shape[1]
            right = block[:, :, at].reshape(deep, width)
            more = jnp.dot(left_ref[:, start : start + deep], right, preferred_element_type=jnp.float32)
            acc = more if acc is None else acc + more
        acc = acc.reshape(2, 512, width)
        if last:
            line = lax.broadcasted_iota(jnp.int32, acc.shape, 1)
            out_ref[...] = jnp.where(line < live_ref[0], acc, 0.0)
        else:
            out_ref[:, :, at] = acc

    if last:
        columns(pl.program_id(0))
    else:
        pl.loop(0, 1024 // width)(columns)


def product(live, left, starts, blocks, total, last, flops=10**6, width=512):
    count = len(blocks)
    first = total is None
    arrays = [near(a) for a in [left, *blocks] + ([] if first else [total])]
    shape = (2, 512, 1024)
    if last:
        out = dict(
            grid=(1024 // width,),
            out_specs=pl.BlockSpec((2, 512, width), lambda n: (0, 0, n)),
            out_shape=jax.ShapeDtypeStruct(shape, jnp.float32),
        )
    else:
        out = dict(
            out_specs=[VMEM] * 2,
            out_shape=[pltpu.VMEM(shape, jnp.float32), TOKEN],
        )
        if not first:
            out["input_output_aliases"] = {2 + count: 0}
    return pl.pallas_call(
        functools.partial(product_kernel, first, last, starts, width),
        in_specs=[SMEM] + [VMEM] * len(arrays),
        compiler_params=pltpu.CompilerParams(vmem_limit_bytes=16 * MIB),
        cost_estimate=pl.CostEstimate(flops=flops, bytes_accessed=MIB, transcendentals=0),
        **out,
    )(live, *arrays)


def along_x(first, second):
    pairs = []
    for y in range(NY):
        for z in range(NZ):
            for x in range(NX):
                for c, step in enumerate((first, second)):
                    pairs.append((index(x + step, y, z, c), index(x, y, z, c)))
    return pairs


def choose(mine, theirs):
    return jnp.where(lax.axis_index("blk") % 2 == 0, mine, theirs)


def pack_kernel(coeffs_ref, mine_ref, theirs_ref, out_ref):
    mine, theirs = mine_ref[...], theirs_ref[...]
    entries = jnp.concatenate([choose(mine, theirs), choose(theirs, mine)], 1).astype(jnp.bfloat16)
    out_ref[:, :, :1024] = coeffs_ref[...]
    out_ref[0, :, 1024:] = entries
    out_ref[1, :, 1024:] = jnp.zeros_like(entries)


def pack(coeffs, mine, theirs):
    return pl.pallas_call(
        pack_kernel,
        in_specs=[VMEM] * 3,
        out_specs=VMEM,
        out_shape=pltpu.VMEM((2, 8, 1152), jnp.bfloat16),
        compiler_params=pltpu.CompilerParams(vmem_limit_bytes=2 * MIB),
        cost_estimate=pl.CostEstimate(flops=0, bytes_accessed=1 << 16, transcendentals=0),
    )(coeffs, mine, theirs)


def unpack_kernel(*refs):
    pieces, slab_ref, table_ref = refs[:4], refs[-2], refs[-1]
    for k, piece in enumerate(pieces):
        slab_ref[:, k * 16 : k * 16 + 16, :] = piece[:, :, :1024]
        table_ref[k * 16 : k * 16 + 16, :] = piece[0, :, 1024:].astype(jnp.float32)


def unpack(pieces, after):
    return pl.pallas_call(
        unpack_kernel,
        in_specs=[VMEM] * 4 + [ANY],
        out_specs=[VMEM] * 2,
        out_shape=[pltpu.VMEM((2, 64, 1024), jnp.bfloat16), pltpu.VMEM((64, 128), jnp.float32)],
        compiler_params=pltpu.CompilerParams(vmem_limit_bytes=2 * MIB),
        cost_estimate=pl.CostEstimate(flops=0, bytes_accessed=MIB, transcendentals=0),
    )(*[near(piece) for piece in pieces], after)


def pick_kernel(mine_ref, theirs_ref, out_ref):
    out_ref[...] = choose(mine_ref[...], theirs_ref[...])


def pick(mine, theirs):
    return pl.pallas_call(
        pick_kernel,
        in_specs=[VMEM] * 2,
        out_specs=VMEM,
        out_shape=pltpu.VMEM((64, 128), jnp.float32),
        compiler_params=pltpu.CompilerParams(vmem_limit_bytes=2 * MIB),
        cost_estimate=pl.CostEstimate(flops=0, bytes_accessed=1 << 16, transcendentals=0),
    )(near(mine), near(theirs))


def gather_tables(table):
    table = pick(table, swap(table))
    side = lax.ppermute(table, AXES, along_x(1, -1))
    return [table, side, swap(side), lax.ppermute(table, AXES, along_x(2, 2))]


def on_device(coeffs, coupling, one_body, target_orb, source_orb, excite, live_rows):
    signs, token = split_cores(coupling, source_orb[None, :], excite)
    row = one_body.reshape(8, 64)
    packed = pack(coeffs, row, swap(row))
    packed = join([packed] + fetch(packed, 0), [(0, 1)], [token])[0]
    arranged, token = arrange(ORDER, signs)
    slab, table = unpack([packed] + fetch(packed, 1), token)
    tables = gather_tables(table)
    halves = list(
        join([slab] + fetch(slab, 2), [(0, 1), (2, 3), (2, 3)], [near(tables[1]), near(tables[3])])
    )
    spare = halves.pop()
    left, token = lookup(target_orb[None, :], tables, arranged, halves[0])
    late = relay(spare, token)

    got = [fetch(halves[0], 3)]
    got.append([lax.ppermute(h, AXES, route(o)) for h, o in zip((halves[1], halves[1], late), STAGES[3])])
    own = halves + [swap(half) for half in halves]
    total, token = product(live_rows, left, (0, 256, 2048, 2304), own, None, False)
    first = join(got[0], [(0, 1, 2)], [token])[0]
    their_first = swap(first)
    total, token = product(live_rows, left, (512,), [first], total, False)
    second = join(got[1], [(0, 1, 2)], [token])[0]
    their_second = swap(second)
    total, _ = product(live_rows, left, (2560, 1280), [their_first, second], total, False)
    return product(live_rows, left, (3328,), [their_second], total, True)


def solution(mesh):
    from jax.sharding import PartitionSpec as P

    return jax.shard_map(
        on_device,
        mesh=mesh,
        in_specs=(
            P(None, ("grp", "blk"), None),
            P(),
            P("grp", None, None, "blk", None),
            P(("grp", "blk")),
            P(),
            P(("grp", "blk"), None),
            P(("grp", "blk")),
        ),
        out_specs=P(None, ("grp", "blk"), None),
        check_vma=False,
    )
```

```python
import functools

import jax
import jax.numpy as jnp
import numpy as np
from jax import lax
from jax.experimental import pallas as pl
from jax.experimental.pallas import tpu as pltpu

NY, NZ, NX = 4, 8, 4
AXES = ("grp", "blk")
STAGES = (
    ((0, 0, 4),),
    ((2, 0, 1), (0, 0, 2), (2, 0, -1)),
    ((0, 1, 1), (0, 2, 0), (0, -1, 1)),
    ((1, 0, 0), (-1, 0, 0), (0, 0, 1)),
)
HERE = ((0, 0, 0),)
SWAP = [(i, i ^ 1) for i in range(NY * NZ * NX * 2)]
MIB = 1 << 20


def mirrored(o):
    return (o[1], o[0], -o[2])


def index(x, y, z, c):
    return ((y % NY * NZ + z % NZ) * NX + x % NX) * 2 + c


def route(offset):
    pairs = []
    for y in range(NY):
        for z in range(NZ):
            for x in range(NX):
                for c in range(2):
                    dx, dy, dz = mirrored(offset) if c else offset
                    pairs.append((index(x + dx, y + dy, z + dz, c), index(x, y, z, c)))
    return pairs


def fetch(block, stage):
    return [lax.ppermute(block, AXES, route(o)) for o in STAGES[stage]]


def swap(block):
    return lax.ppermute(block, AXES, SWAP)


def half_offsets(last, half):
    second = HERE + STAGES[2]
    out = []
    for o2 in second[2 * half : 2 * half + 2]:
        for o1 in HERE + STAGES[1]:
            for o0 in HERE + STAGES[0]:
                out.append([sum(t) for t in zip(last, o2, o1, o0)])
    return out


def order_constants():
    lasts = HERE + STAGES[3]
    own = [(o, h) for o in lasts for h in (0, 1)]
    table = np.zeros((2, 4, 8, 1, 256), np.int32)
    for core in (0, 1):
        for pair in range(8):
            sibling, first = divmod(pair, 4)
            offsets = []
            for last, half in own[2 * first : 2 * first + 2]:
                offsets += half_offsets(last, half)
            offsets = [mirrored(o) if core ^ sibling else o for o in offsets]
            table[core, :3, pair, 0] = np.repeat(np.array(offsets), 8, 0).T
            table[core, 3, pair, 0] = np.tile(np.arange(8), 32)
    return table


ORDER = order_constants()
VMEM = pl.BlockSpec(memory_space=pltpu.VMEM)
SMEM = pl.BlockSpec(memory_space=pltpu.SMEM)
ANY = pl.BlockSpec(memory_space=pl.ANY)
TOKEN = jax.ShapeDtypeStruct((8, 128), jnp.float32)


def near(x):
    return pltpu.with_memory_space_constraint(x, pltpu.VMEM)


def split_kernel(coupling_ref, source_ref, excite_ref, out_ref, token_ref, tiles, labels, couples, sems):
    token_ref[...] = jnp.zeros_like(token_ref)
    small = [
        pltpu.make_async_copy(coupling_ref, couples, sems.at[8]),
        pltpu.make_async_copy(source_ref, labels, sems.at[9]),
    ]
    for copy in small:
        copy.start()
    copies = []
    for tile in range(8):
        part = excite_ref.at[:, tile * 256 : tile * 256 + 256]
        copies.append(pltpu.make_async_copy(part, tiles.at[tile], sems.at[tile]))
        copies[-1].start()
    lane = lax.broadcasted_iota(jnp.int32, (256, 256), 0)
    goal = lax.broadcasted_iota(jnp.int32, (256, 256), 1)
    source = goal % 128 // 8 * 16 + goal // 128 * 8 + goal % 8
    move = (lane == source).astype(jnp.float32).astype(jnp.bfloat16)
    line = lax.broadcasted_iota(jnp.int32, (16, 256), 0)
    for copy in small:
        copy.wait()
    for tile in range(8):
        couple = couples[lax.axis_index("grp"), tile // 2]
        label = labels[:, tile * 256 : tile * 256 + 256] + tile // 2 * 64
        extra = jnp.where(line == 0, label, jnp.where(line == 1, couple, 0))
        copies[tile].wait()
        both = jnp.concatenate([tiles[tile], extra], 0).astype(jnp.float32).astype(jnp.bfloat16)
        moved = jnp.dot(both, move, preferred_element_type=jnp.float32).astype(jnp.bfloat16)
        out_ref[0, :, tile * 128 : tile * 128 + 128] = moved[:, :128]
        out_ref[1, :, tile * 128 : tile * 128 + 128] = moved[:, 128:]


def split_cores(coupling, source, excite):
    return pl.pallas_call(
        split_kernel,
        in_specs=[ANY] * 3,
        out_specs=[VMEM] * 2,
        out_shape=[pltpu.VMEM((2, 528, 1024), jnp.bfloat16), TOKEN],
        scratch_shapes=[
            pltpu.VMEM((8, 512, 256), jnp.int32),
            pltpu.VMEM((1, 2048), jnp.int32),
            pltpu.SMEM((4, 4), jnp.int32),
            pltpu.SemaphoreType.DMA((10,)),
        ],
        compiler_params=pltpu.CompilerParams(vmem_limit_bytes=16 * MIB),
        cost_estimate=pl.CostEstimate(flops=2 * 528 * 2048 * 256, bytes_accessed=7 * MIB, transcendentals=0),
    )(*[pltpu.with_memory_space_constraint(a, pltpu.HBM) for a in (coupling, source, excite)])


def arrange_kernel(order_ref, signs_ref, out_ref, token_ref):
    token_ref[...] = jnp.zeros_like(token_ref)
    blk, core = lax.axis_index("blk"), lax.axis_index("blk") % 2
    y, z, x = lax.axis_index("grp"), blk // 8, blk // 2 % 4

    @pl.loop(0, 8)
    def _(pair):
        dx, dy, dz, place = (jnp.where(core == 0, order_ref[0, i, pair], order_ref[1, i, pair]) for i in range(4))
        chip = (((y + dy) & 3) * NZ + ((z + dz) & 7)) * NX + ((x + dx) & 3)
        line = lax.broadcasted_iota(jnp.int32, (1024, 256), 0)
        move = (line == chip * 8 + place).astype(jnp.float32).astype(jnp.bfloat16)
        owner = jnp.where(pair < 4, core, 1 - core)
        moved = jnp.dot(signs_ref[owner], move, preferred_element_type=jnp.float32)
        out_ref[pair] = moved.astype(jnp.bfloat16)


def arrange(order, signs):
    return pl.pallas_call(
        arrange_kernel,
        in_specs=[VMEM] * 2,
        out_specs=[VMEM] * 2,
        out_shape=[pltpu.VMEM((8, 528, 256), jnp.bfloat16), TOKEN],
        compiler_params=pltpu.CompilerParams(vmem_limit_bytes=16 * MIB),
        cost_estimate=pl.CostEstimate(flops=2 * 528 * 2048 * 1024, bytes_accessed=4 * MIB, transcendentals=0),
    )(order, near(signs))


def table_labels(shape):
    blk = lax.axis_index("blk")
    core, z, x = blk % 2, blk // 8, blk // 2 % 4
    row = lax.broadcasted_iota(jnp.int32, shape, 0)
    along, owner, chip = row >> 4, (row >> 3) & 1, row & 7
    side = 1 + 2 * core
    dx = jnp.where(along == 1, side, jnp.where(along == 2, 4 - side, jnp.where(along == 3, 2, 0)))
    second, first = chip >> 1, chip & 1
    dx = dx + 2 * (second & 1)
    dz = 4 * first + jnp.where(second == 3, 7, second)
    return ((z + dz) & 7) * 8 + ((x + dx) & 3) * 2 + owner


def lookup_kernel(target_ref, signs_ref, after_ref, *refs):
    del after_ref
    tables, (out_ref, token_ref, rows) = refs[:4], refs[4:]
    token_ref[...] = jnp.zeros_like(token_ref)
    hot = (table_labels((64, 512)) == target_ref[...]).astype(jnp.float32).astype(jnp.bfloat16)
    entries = [ref[...].reshape(8, 8, 128) for ref in tables]
    for part in range(2):
        lines = [
            jnp.concatenate([entry[:, 2 * h + part, core * 64 : core * 64 + 64] for h in range(4)], 1)
            for entry in entries
            for core in range(2)
        ]
        table = jnp.concatenate(lines, 0).astype(jnp.bfloat16)
        row = lax.dot_general(hot, table, (((0,), (0,)), ((), ())), preferred_element_type=jnp.float32)
        rows[part * 512 : part * 512 + 512, :] = row.astype(jnp.bfloat16)

    for pair in range(8):
        lines = lax.broadcasted_iota(jnp.int32, (256, 256), 0)
        extra = signs_ref[pair, 512:528, :].astype(jnp.float32)
        label = extra[0:1, :].astype(jnp.int32)
        choice = jnp.where(lines == label, extra[1:2, :], 0.0).astype(jnp.bfloat16)
        look = jnp.dot(rows[...], choice, preferred_element_type=jnp.float32).astype(jnp.bfloat16)
        sign = signs_ref[pair, 0:512, :]
        real, imag = look[:512] * sign, look[512:] * sign
        for half in range(2):
            at, step = column(2 * pair + half)
            piece = slice(half * 128, half * 128 + 128)
            out_ref[:512, at : at + 128] = real[:, piece]
            out_ref[:512, at + step : at + step + 128] = -imag[:, piece]
            out_ref[512:, at : at + 128] = imag[:, piece]
            out_ref[512:, at + step : at + step + 128] = real[:, piece]


def column(chunk):
    return chunk // 2 * 512 + chunk % 2 * 128, 256


def lookup(target, tables, signs, after):
    return pl.pallas_call(
        lookup_kernel,
        in_specs=[VMEM] * 7,
        out_specs=[VMEM] * 2,
        out_shape=[pltpu.VMEM((1024, 4096), jnp.bfloat16), TOKEN],
        scratch_shapes=[pltpu.VMEM((1024, 256), jnp.bfloat16)],
        compiler_params=pltpu.CompilerParams(vmem_limit_bytes=16 * MIB),
        cost_estimate=pl.CostEstimate(flops=10**6, bytes_accessed=MIB, transcendentals=0),
    )(target, *[near(a) for a in (signs, after, *tables)])


def join_kernel(groups, *refs):
    for group, out_ref in zip(groups, refs[len(refs) - len(groups) :]):
        pieces = [refs[k] for k in group]
        if pieces[0].shape[1] % 16:
            out_ref[...] = jnp.concatenate([piece[...] for piece in pieces], 1)
            continue
        at = 0
        for piece in pieces:
            out_ref[:, at : at + piece.shape[1], :] = piece[...]
            at += piece.shape[1]


def join(pieces, groups, after=()):
    shapes = [(2, sum(pieces[k].shape[1] for k in group), pieces[0].shape[2]) for group in groups]
    return pl.pallas_call(
        functools.partial(join_kernel, groups),
        in_specs=[VMEM] * (len(pieces) + len(after)),
        out_specs=[VMEM] * len(groups),
        out_shape=[pltpu.VMEM(shape, jnp.bfloat16) for shape in shapes],
        compiler_params=pltpu.CompilerParams(vmem_limit_bytes=4 * MIB),
        cost_estimate=pl.CostEstimate(flops=0, bytes_accessed=MIB, transcendentals=0),
    )(*[near(p) for p in pieces], *after)


def relay_kernel(*refs):
    del refs


def relay(blocks, after):
    return pl.pallas_call(
        relay_kernel,
        in_specs=[VMEM] * (len(blocks) + 1),
        out_specs=[VMEM] * len(blocks),
        out_shape=[pltpu.VMEM(block.shape, block.dtype) for block in blocks],
        input_output_aliases={k: k for k in range(len(blocks))},
        compiler_params=pltpu.CompilerParams(vmem_limit_bytes=2 * MIB),
        cost_estimate=pl.CostEstimate(flops=0, bytes_accessed=0, transcendentals=0),
    )(*[near(block) for block in blocks], after)


def product_kernel(first, last, starts, width, *refs):
    live_ref, left_ref = refs[:2]
    blocks = refs[2 : 2 + len(starts)]
    total_ref = None if first else refs[2 + len(starts)]
    out_ref = refs[-1 - (not last)]
    if not last:
        refs[-1][...] = jnp.zeros_like(refs[-1])

    def columns(n):
        at = pl.ds(pl.multiple_of(n * width, width), width)
        acc = None if first else total_ref[:, :, at].reshape(1024, width)
        for start, block in zip(starts, blocks):
            deep = 2 * block.shape[1]
            right = block[:, :, at].reshape(deep, width)
            more = jnp.dot(left_ref[:, start : start + deep], right, preferred_element_type=jnp.float32)
            acc = more if acc is None else acc + more
        acc = acc.reshape(2, 512, width)
        if last:
            line = lax.broadcasted_iota(jnp.int32, acc.shape, 1)
            out_ref[...] = jnp.where(line < live_ref[0], acc, 0.0)
        else:
            out_ref[:, :, at] = acc

    if last:
        columns(pl.program_id(0))
    else:
        pl.loop(0, 1024 // width)(columns)


def product(live, left, starts, blocks, total, last, flops=10**6, width=512):
    count = len(blocks)
    first = total is None
    arrays = [near(a) for a in [left, *blocks] + ([] if first else [total])]
    shape = (2, 512, 1024)
    if last:
        out = dict(
            grid=(1024 // width,),
            out_specs=pl.BlockSpec((2, 512, width), lambda n: (0, 0, n)),
            out_shape=jax.ShapeDtypeStruct(shape, jnp.float32),
        )
    else:
        out = dict(
            out_specs=[VMEM] * 2,
            out_shape=[pltpu.VMEM(shape, jnp.float32), TOKEN],
        )
        if not first:
            out["input_output_aliases"] = {2 + count: 0}
    return pl.pallas_call(
        functools.partial(product_kernel, first, last, starts, width),
        in_specs=[SMEM] + [VMEM] * len(arrays),
        compiler_params=pltpu.CompilerParams(vmem_limit_bytes=16 * MIB),
        cost_estimate=pl.CostEstimate(flops=flops, bytes_accessed=MIB, transcendentals=0),
        **out,
    )(live, *arrays)


def along_x(first, second):
    pairs = []
    for y in range(NY):
        for z in range(NZ):
            for x in range(NX):
                for c, step in enumerate((first, second)):
                    pairs.append((index(x + step, y, z, c), index(x, y, z, c)))
    return pairs


def choose(mine, theirs):
    return jnp.where(lax.axis_index("blk") % 2 == 0, mine, theirs)


def pack_kernel(coeffs_ref, mine_ref, theirs_ref, out_ref):
    mine, theirs = mine_ref[...], theirs_ref[...]
    entries = jnp.concatenate([choose(mine, theirs), choose(theirs, mine)], 1).astype(jnp.bfloat16)
    out_ref[:, :, :1024] = coeffs_ref[...]
    out_ref[0, :, 1024:] = entries
    out_ref[1, :, 1024:] = jnp.zeros_like(entries)


def pack(coeffs, mine, theirs):
    return pl.pallas_call(
        pack_kernel,
        in_specs=[VMEM] * 3,
        out_specs=VMEM,
        out_shape=pltpu.VMEM((2, 8, 1152), jnp.bfloat16),
        compiler_params=pltpu.CompilerParams(vmem_limit_bytes=2 * MIB),
        cost_estimate=pl.CostEstimate(flops=0, bytes_accessed=1 << 16, transcendentals=0),
    )(*[pltpu.with_memory_space_constraint(a, pltpu.HBM) for a in (coeffs, mine)], theirs)


def unpack_kernel(*refs):
    pieces, slab_ref, table_ref = refs[:4], refs[-2], refs[-1]
    for k, piece in enumerate(pieces):
        slab_ref[:, k * 16 : k * 16 + 16, :] = piece[:, :, :1024]
        table_ref[k * 16 : k * 16 + 16, :] = piece[0, :, 1024:].astype(jnp.float32)


def unpack(pieces, after):
    return pl.pallas_call(
        unpack_kernel,
        in_specs=[VMEM] * 4 + [ANY],
        out_specs=[VMEM] * 2,
        out_shape=[pltpu.VMEM((2, 64, 1024), jnp.bfloat16), pltpu.VMEM((64, 128), jnp.float32)],
        compiler_params=pltpu.CompilerParams(vmem_limit_bytes=2 * MIB),
        cost_estimate=pl.CostEstimate(flops=0, bytes_accessed=MIB, transcendentals=0),
    )(*[near(piece) for piece in pieces], after)


def pick_kernel(mine_ref, theirs_ref, out_ref):
    out_ref[...] = choose(mine_ref[...], theirs_ref[...])


def pick(mine, theirs):
    return pl.pallas_call(
        pick_kernel,
        in_specs=[VMEM] * 2,
        out_specs=VMEM,
        out_shape=pltpu.VMEM((64, 128), jnp.float32),
        compiler_params=pltpu.CompilerParams(vmem_limit_bytes=2 * MIB),
        cost_estimate=pl.CostEstimate(flops=0, bytes_accessed=1 << 16, transcendentals=0),
    )(near(mine), near(theirs))


def gather_tables(table):
    table = pick(table, swap(table))
    side = lax.ppermute(table, AXES, along_x(1, -1))
    return [table, side, swap(side), lax.ppermute(table, AXES, along_x(2, 2))]


def on_device(coeffs, coupling, one_body, target_orb, source_orb, excite, live_rows):
    signs, token = split_cores(coupling, source_orb[None, :], excite)
    row = one_body.reshape(8, 64)
    packed = pack(coeffs, row, swap(row))
    packed = join([packed] + fetch(packed, 0), [(0, 1)], [token])[0]
    arranged, token = arrange(ORDER, signs)
    slab, table = unpack([packed] + fetch(packed, 1), token)
    tables = gather_tables(table)
    slab = join([slab] + fetch(slab, 2), [(0, 1, 2, 3)], [near(tables[1]), near(tables[3])])[0]
    left, _ = lookup(target_orb[None, :], tables, arranged, slab)

    got = fetch(slab, 3)
    total, token = product(live_rows, left, (0, 2048), [slab, swap(slab)], None, False)
    third = relay(got[2:], token)[0]
    their_third = swap(third)
    total, token = product(live_rows, left, (1536,), [third], total, False)
    got = [relay([block], token)[0] for block in got[:2]]
    swapped = [swap(block) for block in got]
    total, _ = product(live_rows, left, (512, 1024), got, total, False)
    total, _ = product(live_rows, left, (3584, 3072), [their_third, swapped[1]], total, False)
    return product(live_rows, left, (2560,), swapped[:1], total, True)


def solution(mesh):
    from jax.sharding import PartitionSpec as P

    return jax.shard_map(
        on_device,
        mesh=mesh,
        in_specs=(
            P(None, ("grp", "blk"), None),
            P(),
            P("grp", None, None, "blk", None),
            P(("grp", "blk")),
            P(),
            P(("grp", "blk"), None),
            P(("grp", "blk")),
        ),
        out_specs=P(None, ("grp", "blk"), None),
        check_vma=False,
    )
```

```python
import functools

import jax
import jax.numpy as jnp
import numpy as np
from jax import lax
from jax.experimental import pallas as pl
from jax.experimental.pallas import tpu as pltpu

NY, NZ, NX = 4, 8, 4
AXES = ("grp", "blk")
STAGES = (
    ((0, 0, 4),),
    ((2, 0, 1), (0, 0, 2), (2, 0, -1)),
    ((0, 1, 1), (0, 2, 0), (0, -1, 1)),
    ((1, 0, 0), (-1, 0, 0), (0, 0, 1)),
)
HERE = ((0, 0, 0),)
SWAP = [(i, i ^ 1) for i in range(NY * NZ * NX * 2)]
MIB = 1 << 20


def mirrored(o):
    return (o[1], o[0], -o[2])


def index(x, y, z, c):
    return ((y % NY * NZ + z % NZ) * NX + x % NX) * 2 + c


def route(offset):
    pairs = []
    for y in range(NY):
        for z in range(NZ):
            for x in range(NX):
                for c in range(2):
                    dx, dy, dz = mirrored(offset) if c else offset
                    pairs.append((index(x + dx, y + dy, z + dz, c), index(x, y, z, c)))
    return pairs


def fetch(block, stage):
    return [lax.ppermute(block, AXES, route(o)) for o in STAGES[stage]]


def swap(block):
    return lax.ppermute(block, AXES, SWAP)


def half_offsets(last, half):
    second = HERE + STAGES[2]
    out = []
    for o2 in second[2 * half : 2 * half + 2]:
        for o1 in HERE + STAGES[1]:
            for o0 in HERE + STAGES[0]:
                out.append([sum(t) for t in zip(last, o2, o1, o0)])
    return out


def order_constants():
    lasts = HERE + STAGES[3]
    own = [(o, h) for o in lasts for h in (0, 1)]
    table = np.zeros((2, 4, 8, 1, 256), np.int32)
    for core in (0, 1):
        for pair in range(8):
            sibling, first = divmod(pair, 4)
            offsets = []
            for last, half in own[2 * first : 2 * first + 2]:
                offsets += half_offsets(last, half)
            offsets = [mirrored(o) if core ^ sibling else o for o in offsets]
            table[core, :3, pair, 0] = np.repeat(np.array(offsets), 8, 0).T
            table[core, 3, pair, 0] = np.tile(np.arange(8), 32)
    return table


ORDER = order_constants()
VMEM = pl.BlockSpec(memory_space=pltpu.VMEM)
SMEM = pl.BlockSpec(memory_space=pltpu.SMEM)
ANY = pl.BlockSpec(memory_space=pl.ANY)
TOKEN = jax.ShapeDtypeStruct((8, 128), jnp.float32)


def near(x):
    return pltpu.with_memory_space_constraint(x, pltpu.VMEM)


def split_kernel(coupling_ref, source_ref, excite_ref, out_ref, token_ref, tiles, labels, couples, sems):
    token_ref[...] = jnp.zeros_like(token_ref)
    small = [
        pltpu.make_async_copy(coupling_ref, couples, sems.at[8]),
        pltpu.make_async_copy(source_ref, labels, sems.at[9]),
    ]
    for copy in small:
        copy.start()
    copies = []
    for tile in range(8):
        part = excite_ref.at[:, tile * 256 : tile * 256 + 256]
        copies.append(pltpu.make_async_copy(part, tiles.at[tile], sems.at[tile]))
        copies[-1].start()
    lane = lax.broadcasted_iota(jnp.int32, (256, 256), 0)
    goal = lax.broadcasted_iota(jnp.int32, (256, 256), 1)
    source = goal % 128 // 8 * 16 + goal // 128 * 8 + goal % 8
    move = (lane == source).astype(jnp.float32).astype(jnp.bfloat16)
    line = lax.broadcasted_iota(jnp.int32, (16, 256), 0)
    for copy in small:
        copy.wait()
    for tile in range(8):
        couple = couples[lax.axis_index("grp"), tile // 2]
        label = labels[:, tile * 256 : tile * 256 + 256] + tile // 2 * 64
        extra = jnp.where(line == 0, label, jnp.where(line == 1, couple, 0))
        copies[tile].wait()
        both = jnp.concatenate([tiles[tile], extra], 0).astype(jnp.float32).astype(jnp.bfloat16)
        moved = jnp.dot(both, move, preferred_element_type=jnp.float32).astype(jnp.bfloat16)
        out_ref[0, :, tile * 128 : tile * 128 + 128] = moved[:, :128]
        out_ref[1, :, tile * 128 : tile * 128 + 128] = moved[:, 128:]


def split_cores(coupling, source, excite):
    return pl.pallas_call(
        split_kernel,
        in_specs=[ANY] * 3,
        out_specs=[VMEM] * 2,
        out_shape=[pltpu.VMEM((2, 528, 1024), jnp.bfloat16), TOKEN],
        scratch_shapes=[
            pltpu.VMEM((8, 512, 256), jnp.int32),
            pltpu.VMEM((1, 2048), jnp.int32),
            pltpu.SMEM((4, 4), jnp.int32),
            pltpu.SemaphoreType.DMA((10,)),
        ],
        compiler_params=pltpu.CompilerParams(vmem_limit_bytes=16 * MIB),
        cost_estimate=pl.CostEstimate(flops=2 * 528 * 2048 * 256, bytes_accessed=7 * MIB, transcendentals=0),
    )(*[pltpu.with_memory_space_constraint(a, pltpu.HBM) for a in (coupling, source, excite)])


def arrange_kernel(order_ref, signs_ref, out_ref, token_ref):
    token_ref[...] = jnp.zeros_like(token_ref)
    blk, core = lax.axis_index("blk"), lax.axis_index("blk") % 2
    y, z, x = lax.axis_index("grp"), blk // 8, blk // 2 % 4

    @pl.loop(0, 8)
    def _(pair):
        dx, dy, dz, place = (jnp.where(core == 0, order_ref[0, i, pair], order_ref[1, i, pair]) for i in range(4))
        chip = (((y + dy) & 3) * NZ + ((z + dz) & 7)) * NX + ((x + dx) & 3)
        line = lax.broadcasted_iota(jnp.int32, (1024, 256), 0)
        move = (line == chip * 8 + place).astype(jnp.float32).astype(jnp.bfloat16)
        owner = jnp.where(pair < 4, core, 1 - core)
        moved = jnp.dot(signs_ref[owner], move, preferred_element_type=jnp.float32)
        out_ref[pair] = moved.astype(jnp.bfloat16)


def arrange(order, signs):
    return pl.pallas_call(
        arrange_kernel,
        in_specs=[VMEM] * 2,
        out_specs=[VMEM] * 2,
        out_shape=[pltpu.VMEM((8, 528, 256), jnp.bfloat16), TOKEN],
        compiler_params=pltpu.CompilerParams(vmem_limit_bytes=16 * MIB),
        cost_estimate=pl.CostEstimate(flops=2 * 528 * 2048 * 1024, bytes_accessed=4 * MIB, transcendentals=0),
    )(order, near(signs))


def table_labels(shape):
    blk = lax.axis_index("blk")
    core, z, x = blk % 2, blk // 8, blk // 2 % 4
    row = lax.broadcasted_iota(jnp.int32, shape, 0)
    along, owner, chip = row >> 4, (row >> 3) & 1, row & 7
    side = 1 + 2 * core
    dx = jnp.where(along == 1, side, jnp.where(along == 2, 4 - side, jnp.where(along == 3, 2, 0)))
    second, first = chip >> 1, chip & 1
    dx = dx + 2 * (second & 1)
    dz = 4 * first + jnp.where(second == 3, 7, second)
    return ((z + dz) & 7) * 8 + ((x + dx) & 3) * 2 + owner


def lookup_kernel(target_ref, signs_ref, after_ref, *refs):
    del after_ref
    tables, (out_ref, token_ref, rows) = refs[:4], refs[4:]
    token_ref[...] = jnp.zeros_like(token_ref)
    hot = (table_labels((64, 512)) == target_ref[...]).astype(jnp.float32).astype(jnp.bfloat16)
    entries = [ref[...].reshape(8, 8, 128) for ref in tables]
    for part in range(2):
        lines = [
            jnp.concatenate([entry[:, 2 * h + part, core * 64 : core * 64 + 64] for h in range(4)], 1)
            for entry in entries
            for core in range(2)
        ]
        table = jnp.concatenate(lines, 0).astype(jnp.bfloat16)
        row = lax.dot_general(hot, table, (((0,), (0,)), ((), ())), preferred_element_type=jnp.float32)
        rows[part * 512 : part * 512 + 512, :] = row.astype(jnp.bfloat16)

    for pair in range(8):
        lines = lax.broadcasted_iota(jnp.int32, (256, 256), 0)
        extra = signs_ref[pair, 512:528, :].astype(jnp.float32)
        label = extra[0:1, :].astype(jnp.int32)
        choice = jnp.where(lines == label, extra[1:2, :], 0.0).astype(jnp.bfloat16)
        look = jnp.dot(rows[...], choice, preferred_element_type=jnp.float32).astype(jnp.bfloat16)
        sign = signs_ref[pair, 0:512, :]
        real, imag = look[:512] * sign, look[512:] * sign
        for half in range(2):
            at, step = column(2 * pair + half)
            piece = slice(half * 128, half * 128 + 128)
            out_ref[:512, at : at + 128] = real[:, piece]
            out_ref[:512, at + step : at + step + 128] = -imag[:, piece]
            out_ref[512:, at : at + 128] = imag[:, piece]
            out_ref[512:, at + step : at + step + 128] = real[:, piece]


def column(chunk):
    return chunk // 2 * 512 + chunk % 2 * 128, 256


def lookup(target, tables, signs, after):
    return pl.pallas_call(
        lookup_kernel,
        in_specs=[VMEM] * 7,
        out_specs=[VMEM] * 2,
        out_shape=[pltpu.VMEM((1024, 4096), jnp.bfloat16), TOKEN],
        scratch_shapes=[pltpu.VMEM((1024, 256), jnp.bfloat16)],
        compiler_params=pltpu.CompilerParams(vmem_limit_bytes=16 * MIB),
        cost_estimate=pl.CostEstimate(flops=10**6, bytes_accessed=MIB, transcendentals=0),
    )(target, *[near(a) for a in (signs, after, *tables)])


def join_kernel(groups, *refs):
    for group, out_ref in zip(groups, refs[len(refs) - len(groups) :]):
        pieces = [refs[k] for k in group]
        if pieces[0].shape[1] % 16:
            out_ref[...] = jnp.concatenate([piece[...] for piece in pieces], 1)
            continue
        at = 0
        for piece in pieces:
            out_ref[:, at : at + piece.shape[1], :] = piece[...]
            at += piece.shape[1]


def join(pieces, groups, after=()):
    shapes = [(2, sum(pieces[k].shape[1] for k in group), pieces[0].shape[2]) for group in groups]
    return pl.pallas_call(
        functools.partial(join_kernel, groups),
        in_specs=[VMEM] * (len(pieces) + len(after)),
        out_specs=[VMEM] * len(groups),
        out_shape=[pltpu.VMEM(shape, jnp.bfloat16) for shape in shapes],
        compiler_params=pltpu.CompilerParams(vmem_limit_bytes=4 * MIB),
        cost_estimate=pl.CostEstimate(flops=0, bytes_accessed=MIB, transcendentals=0),
    )(*[near(p) for p in pieces], *after)


def relay_kernel(*refs):
    del refs


def relay(blocks, after):
    return pl.pallas_call(
        relay_kernel,
        in_specs=[VMEM] * (len(blocks) + 1),
        out_specs=[VMEM] * len(blocks),
        out_shape=[pltpu.VMEM(block.shape, block.dtype) for block in blocks],
        input_output_aliases={k: k for k in range(len(blocks))},
        compiler_params=pltpu.CompilerParams(vmem_limit_bytes=2 * MIB),
        cost_estimate=pl.CostEstimate(flops=0, bytes_accessed=0, transcendentals=0),
    )(*[near(block) for block in blocks], after)


def product_kernel(first, last, starts, width, *refs):
    live_ref, left_ref = refs[:2]
    blocks = refs[2 : 2 + len(starts)]
    total_ref = None if first else refs[2 + len(starts)]
    out_ref = refs[-1 - (not last)]
    if not last:
        refs[-1][...] = jnp.zeros_like(refs[-1])

    def columns(n):
        at = pl.ds(pl.multiple_of(n * width, width), width)
        acc = None if first else total_ref[:, :, at].reshape(1024, width)
        for start, block in zip(starts, blocks):
            deep = 2 * block.shape[1]
            right = block[:, :, at].reshape(deep, width)
            more = jnp.dot(left_ref[:, start : start + deep], right, preferred_element_type=jnp.float32)
            acc = more if acc is None else acc + more
        acc = acc.reshape(2, 512, width)
        if last:
            line = lax.broadcasted_iota(jnp.int32, acc.shape, 1)
            out_ref[...] = jnp.where(line < live_ref[0], acc, 0.0)
        else:
            out_ref[:, :, at] = acc

    if last:
        columns(pl.program_id(0))
    else:
        pl.loop(0, 1024 // width)(columns)


def product(live, left, starts, blocks, total, last, flops=10**6, width=512):
    count = len(blocks)
    first = total is None
    arrays = [near(a) for a in [left, *blocks] + ([] if first else [total])]
    shape = (2, 512, 1024)
    if last:
        out = dict(
            grid=(1024 // width,),
            out_specs=pl.BlockSpec((2, 512, width), lambda n: (0, 0, n)),
            out_shape=jax.ShapeDtypeStruct(shape, jnp.float32),
        )
    else:
        out = dict(
            out_specs=[VMEM] * 2,
            out_shape=[pltpu.VMEM(shape, jnp.float32), TOKEN],
        )
        if not first:
            out["input_output_aliases"] = {2 + count: 0}
    return pl.pallas_call(
        functools.partial(product_kernel, first, last, starts, width),
        in_specs=[SMEM] + [VMEM] * len(arrays),
        compiler_params=pltpu.CompilerParams(vmem_limit_bytes=16 * MIB),
        cost_estimate=pl.CostEstimate(flops=flops, bytes_accessed=MIB, transcendentals=0),
        **out,
    )(live, *arrays)


def along_x(first, second):
    pairs = []
    for y in range(NY):
        for z in range(NZ):
            for x in range(NX):
                for c, step in enumerate((first, second)):
                    pairs.append((index(x + step, y, z, c), index(x, y, z, c)))
    return pairs


def choose(mine, theirs):
    return jnp.where(lax.axis_index("blk") % 2 == 0, mine, theirs)


def pack_kernel(coeffs_ref, mine_ref, theirs_ref, out_ref):
    mine, theirs = mine_ref[...], theirs_ref[...]
    entries = jnp.concatenate([choose(mine, theirs), choose(theirs, mine)], 1).astype(jnp.bfloat16)
    out_ref[:, :, :1024] = coeffs_ref[...]
    out_ref[0, :, 1024:] = entries
    out_ref[1, :, 1024:] = jnp.zeros_like(entries)


def pack(coeffs, mine, theirs):
    return pl.pallas_call(
        pack_kernel,
        in_specs=[VMEM] * 3,
        out_specs=VMEM,
        out_shape=pltpu.VMEM((2, 8, 1152), jnp.bfloat16),
        compiler_params=pltpu.CompilerParams(vmem_limit_bytes=2 * MIB),
        cost_estimate=pl.CostEstimate(flops=0, bytes_accessed=1 << 16, transcendentals=0),
    )(*[pltpu.with_memory_space_constraint(a, pltpu.HBM) for a in (coeffs, mine)], theirs)


def unpack_kernel(*refs):
    pieces, slab_ref, table_ref = refs[:4], refs[-2], refs[-1]
    for k, piece in enumerate(pieces):
        slab_ref[:, k * 16 : k * 16 + 16, :] = piece[:, :, :1024]
        table_ref[k * 16 : k * 16 + 16, :] = piece[0, :, 1024:].astype(jnp.float32)


def unpack(pieces, after):
    return pl.pallas_call(
        unpack_kernel,
        in_specs=[VMEM] * 4 + [ANY],
        out_specs=[VMEM] * 2,
        out_shape=[pltpu.VMEM((2, 64, 1024), jnp.bfloat16), pltpu.VMEM((64, 128), jnp.float32)],
        compiler_params=pltpu.CompilerParams(vmem_limit_bytes=2 * MIB),
        cost_estimate=pl.CostEstimate(flops=0, bytes_accessed=MIB, transcendentals=0),
    )(*[near(piece) for piece in pieces], after)


def pick_kernel(mine_ref, theirs_ref, out_ref):
    out_ref[...] = choose(mine_ref[...], theirs_ref[...])


def pick(mine, theirs):
    return pl.pallas_call(
        pick_kernel,
        in_specs=[VMEM] * 2,
        out_specs=VMEM,
        out_shape=pltpu.VMEM((64, 128), jnp.float32),
        compiler_params=pltpu.CompilerParams(vmem_limit_bytes=2 * MIB),
        cost_estimate=pl.CostEstimate(flops=0, bytes_accessed=1 << 16, transcendentals=0),
    )(near(mine), near(theirs))


def gather_tables(table):
    table = pick(table, swap(table))
    side = lax.ppermute(table, AXES, along_x(1, -1))
    return [table, side, swap(side), lax.ppermute(table, AXES, along_x(2, 2))]


def on_device(coeffs, coupling, one_body, target_orb, source_orb, excite, live_rows):
    signs, token = split_cores(coupling, source_orb[None, :], excite)
    row = one_body.reshape(8, 64)
    packed = pack(coeffs, row, swap(row))
    packed = join([packed] + fetch(packed, 0), [(0, 1)], [token])[0]
    arranged, token = arrange(ORDER, signs)
    slab, table = unpack([packed] + fetch(packed, 1), token)
    tables = gather_tables(table)
    slab = join([slab] + fetch(slab, 2), [(0, 1, 2, 3)], [near(tables[1]), near(tables[3])])[0]
    left, _ = lookup(target_orb[None, :], tables, arranged, slab)

    got = fetch(slab, 3)
    total, token = product(live_rows, left, (0, 2048), [slab, swap(slab)], None, False)
    third = relay(got[2:], token)[0]
    their_third = swap(third)
    total, token = product(live_rows, left, (1536,), [third], total, False)
    got = [relay([block], token)[0] for block in got[:2]]
    swapped = [swap(block) for block in got]
    total, _ = product(live_rows, left, (512, 1024), got, total, False)
    return product(live_rows, left, (3584, 3072, 2560), [their_third, swapped[1], swapped[0]], total, True)


def solution(mesh):
    from jax.sharding import PartitionSpec as P

    return jax.shard_map(
        on_device,
        mesh=mesh,
        in_specs=(
            P(None, ("grp", "blk"), None),
            P(),
            P("grp", None, None, "blk", None),
            P(("grp", "blk")),
            P(),
            P(("grp", "blk"), None),
            P(("grp", "blk")),
        ),
        out_specs=P(None, ("grp", "blk"), None),
        check_vma=False,
    )
```
